32 devices in a mesh: hi: 8 (over y, x, core), lo: 4 (over z).
Axes of the slice: x: 2, y: 2, z: 4, core: 2. Of those that a mesh axis runs over, the one named last changes fastest.
Arguments:
- previous: float32 [32, 524288], P(None, ('hi', 'lo')), may hold values from -6 to 6
- current: float32 [32, 524288], P(None, ('hi', 'lo')), may hold values from -6 to 6
- field_levels: int32 [19], replicated, may hold values from -4 to 4
- bond_levels: int32 [18], replicated, may hold values from 1 to 3
Outputs:
- ortho_block: float32 [32, 524288], P(None, ('hi', 'lo'))
- upper_factor: float32 [32, 32], replicated
The draws below stay inside these ranges and needn't reach their ends.
All inputs are finite; a program needn't handle non-finite values.
Results may differ from the reference program's by a relative error of at most 0.00005.
Values sent between devices are 32-bit elements; how exact they have to be, the bound alone decides.
No kernel may reach another device: no remote copies, remote signals or barrier semaphores. Data moves between devices by JAX's collectives and lax.ppermute only.
A program may use at most 64 MiB of HBM per device.

```python
import jax
import jax.numpy as jnp
from jax import lax

NVEC = 32
LB = 14
GB = 5
SITES = 19
BONDS = 18
DIM = 524288


def place_ends(array, stream_key, low, largest):
    longest = array.shape.index(max(array.shape))
    spots = []
    for shift in (0, 1):
        where = [jax.random.randint(jax.random.fold_in(stream_key, axis), (), 0, length) for axis, length in enumerate(array.shape)]
        where[longest] = (where[longest] + shift) % array.shape[longest]
        spots.append(tuple(where))
    return array.at[spots[0]].set(low).at[spots[1]].set(largest)


def block_scale(key, dims, pieces, low, high):
    def one(dim, blocks):
        draws = jax.random.uniform(jax.random.fold_in(jax.random.fold_in(key, 6), dim), (blocks,), jnp.float32, low / len(pieces), high / len(pieces))
        return jnp.repeat(jnp.exp(draws), dims[dim] // blocks).reshape((-1,) + (1,) * (len(dims) - dim - 1))

    level = one(*pieces[0])
    for cut in pieces[1:]:
        level = level * one(*cut)
    return level


def scatter_about(rng, extent, scale, most, shards=(), kind=jnp.bfloat16):
    array = jax.random.normal(rng, extent, jnp.float32) * scale
    if len(shards) > 0:
        array = block_scale(rng, extent, shards, -0.22, 0.18) * array
    return jnp.clip(array, min=-most, max=most).astype(kind)


def setup_inputs(seed: int = 0) -> dict:
    arg_keys = jax.random.split(jax.random.key(seed), 5)
    previous = scatter_about(arg_keys[0], (NVEC, DIM), 1.0, 6.0, ((1, 32),), jnp.float32)
    current = scatter_about(arg_keys[1], (NVEC, DIM), 1.0, 6.0, ((1, 32),), jnp.float32)
    field_levels = place_ends(jax.random.randint(arg_keys[2], (SITES,), -4, 5), jax.random.fold_in(arg_keys[2], 1), -4, 4).astype(jnp.int32)
    bond_levels = place_ends(jax.random.randint(arg_keys[3], (BONDS,), 1, 4), jax.random.fold_in(arg_keys[3], 1), 1, 3).astype(jnp.int32)
    return {"previous": previous, "current": current, "field_levels": field_levels, "bond_levels": bond_levels}


FIELD_STEP = 0.75
COUPLING_STEP = 0.5

def site_bit(site_number):
    if site_number < GB:
        return LB - GB + site_number
    if site_number < LB:
        return site_number - GB
    return site_number

def pair_flip(values, first_bit, second_bit, bit_count):
    top_bit = max(first_bit, second_bit)
    low_bit = min(first_bit, second_bit)
    vectors = values.shape[0]
    shaped = values.reshape(vectors, 2 ** (bit_count - top_bit - 1), 2, 2 ** (top_bit - low_bit - 1), 2, 2 ** low_bit)
    flipped = jnp.flip(shaped, axis=(2, 4))
    opposite = (1.0 - jnp.eye(2, dtype=jnp.float32)).reshape(1, 1, 2, 1, 2, 1)
    return (flipped * opposite).reshape(values.shape)

def reference(previous, current, field_levels, bond_levels):
    full_index = lax.iota(jnp.int32, DIM)
    spin_values = [0.5 - (full_index >> site_bit(site_number) & 1).astype(jnp.float32) for site_number in range(SITES)]
    fields = FIELD_STEP * field_levels.astype(jnp.float32)
    couplings = COUPLING_STEP * bond_levels.astype(jnp.float32)
    diagonal = jnp.zeros((DIM,), jnp.float32)
    for site_number in range(SITES):
        diagonal = diagonal + fields[site_number] * spin_values[site_number]
        if site_number < SITES - 1:
            diagonal = diagonal + couplings[site_number] * spin_values[site_number] * spin_values[site_number + 1]
    applied = diagonal[None, :] * current
    for site_number in range(SITES - 1):
        applied = applied + 0.5 * couplings[site_number] * pair_flip(current, site_bit(site_number), site_bit(site_number + 1), SITES)
    filtered = 4.0 / SITES * applied - previous
    gram_matrix = jnp.dot(filtered, filtered.T, precision=lax.Precision.HIGHEST) / DIM
    lower_factor = jnp.linalg.cholesky(gram_matrix)
    inverse = jax.scipy.linalg.solve_triangular(lower_factor, jnp.eye(NVEC, dtype=jnp.float32), lower=True)
    ortho_block = jnp.dot(inverse, filtered, precision=lax.Precision.HIGHEST)
    return (ortho_block, lower_factor.T)
```

```python
import functools

import jax
import jax.numpy as jnp
from jax import lax
from jax.experimental import pallas as pl
from jax.experimental.pallas import tpu as pltpu
from jax.sharding import PartitionSpec as P

FIELD_STEP = 0.75
COUPLING_STEP = 0.5
AXES = ("hi", "lo")
LANES = 128
LANE_BITS = 7
GROUP = 256
GROUP_BITS = 8
VMEM_LIMIT = 48 * 1024 * 1024


def pieces(values, count):
    parts = []
    for _ in range(count):
        part = values.astype(jnp.bfloat16)
        parts.append(part)
        values = values - part.astype(jnp.float32)
    return parts


def smem():
    return pl.BlockSpec(memory_space=pltpu.SMEM)


def params():
    return pltpu.CompilerParams(vmem_limit_bytes=VMEM_LIMIT)


def triple_pairs(devices, p, m, q, sum_low):
    def routes(moves):
        table = {}
        for source, target in moves:
            for one, two in ((source, target), (tuple(1 - b for b in source), tuple(1 - b for b in target))):
                table[one] = two
        pairs = []
        for device in range(devices):
            state = (device >> p & 1, device >> m & 1, device >> q & 1)
            if state in table:
                goal = table[state]
                other = device & ~(1 << p | 1 << m | 1 << q)
                pairs.append((device, other | goal[0] << p | goal[1] << m | goal[2] << q))
        return pairs

    site = (0, 1, 0) if sum_low else (1, 1, 1)
    first = routes([((0, 1, 0), (1, 0, 0)), ((1, 1, 0), site)])
    second = routes([(site, (1, 0, 1)), ((1, 0, 0), (0, 0, 1))])
    return first, second, site


def half_kernel(select_ref, x_ref, out_ref, *, span):
    upper = select_ref[0] == 1
    for k in range(out_ref.shape[1] // span):
        lower_part = x_ref[:, 2 * k * span : (2 * k + 1) * span]
        upper_part = x_ref[:, (2 * k + 1) * span : (2 * k + 2) * span]
        out_ref[:, k * span : (k + 1) * span] = jnp.where(upper, upper_part, lower_part)


def take_half(current, select, span):
    vectors, amp_count = current.shape
    steps = 4 if amp_count // (2 * span) % 4 == 0 else 1
    return pl.pallas_call(
        functools.partial(half_kernel, span=span),
        grid=(steps,),
        out_shape=jax.ShapeDtypeStruct((vectors, amp_count // 2), jnp.float32),
        in_specs=[smem(), pl.BlockSpec((vectors, amp_count // steps), lambda i: (0, i))],
        out_specs=pl.BlockSpec((vectors, amp_count // 2 // steps), lambda i: (0, i)),
        compiler_params=params(),
        name="take_half",
    )(select, current)


def local_kernel(weight_ref, x_ref, prev_ref, diag_ref, matrix_ref, out_ref, *, tile_bonds, wraps):
    vectors, amp_count = x_ref.shape
    groups = amp_count // GROUP
    stacked = jnp.concatenate([x_ref[:, k * GROUP : (k + 1) * GROUP] for k in range(groups)], axis=0)
    matrix = matrix_ref[...]
    product = None
    for part in pieces(stacked, 3):
        term = jnp.dot(part, matrix, preferred_element_type=jnp.float32)
        product = term if product is None else product + term
    scale = weight_ref[len(tile_bonds) + len(wraps)]
    lane = lax.broadcasted_iota(jnp.int32, (vectors, LANES), 1)

    def tile(t):
        return x_ref[:, t * LANES : (t + 1) * LANES]

    for t in range(amp_count // LANES):
        row = t // 2 * vectors
        side = (t & 1) * LANES
        total = diag_ref[:, t * LANES : (t + 1) * LANES] * tile(t) - prev_ref[:, t * LANES : (t + 1) * LANES]
        total = total + scale * product[row : row + vectors, side : side + LANES]
        for number, (one, two) in enumerate(tile_bonds):
            if (t >> one & 1) != (t >> two & 1):
                total = total + weight_ref[number] * tile(t ^ (1 << one) ^ (1 << two))
        for number, (high, low) in enumerate(wraps):
            up = t >> high & 1
            shift = 1 << low if up == 0 else LANES - (1 << low)
            moved = pltpu.roll(tile(t ^ (1 << high)), shift, 1)
            total = total + jnp.where((lane >> low & 1) != up, weight_ref[len(tile_bonds) + number] * moved, 0.0)
        out_ref[:, t * LANES : (t + 1) * LANES] = total


def gather_kernel(weight_ref, local_ref, one_ref, two_ref, half_ref, out_ref, *, span):
    first, second = weight_ref[0], weight_ref[1]
    lower, upper = weight_ref[2], weight_ref[3]
    for k in range(half_ref.shape[1] // span):
        part = half_ref[:, k * span : (k + 1) * span]
        for side, weight in ((0, lower), (1, upper)):
            cols = slice((2 * k + side) * span, (2 * k + side + 1) * span)
            out_ref[:, cols] = local_ref[:, cols] + first * one_ref[:, cols] + second * two_ref[:, cols] + weight * part


def filter_kernel(weight_ref, acc_ref, one_ref, two_ref, half_ref, out_ref, gram_ref, total_ref, *, span, scale):
    lower, upper = weight_ref[2], weight_ref[3]
    step = pl.program_id(0)
    vectors = acc_ref.shape[0]

    @pl.when(step == 0)
    def _():
        total_ref[...] = jnp.zeros_like(total_ref)

    for k in range(half_ref.shape[1] // span):
        part = half_ref[:, k * span : (k + 1) * span]
        for side, weight in ((0, lower), (1, upper)):
            cols = slice((2 * k + side) * span, (2 * k + side + 1) * span)
            out_ref[:, cols] = acc_ref[:, cols] + one_ref[:, cols] + two_ref[:, cols] + weight * part
    stacked = jnp.concatenate(pieces(out_ref[...], 3), axis=0)
    total_ref[...] += lax.dot_general(
        stacked, stacked, (((1,), (1,)), ((), ())), preferred_element_type=jnp.float32
    )

    @pl.when(step == pl.num_programs(0) - 1)
    def _():
        table = total_ref[...]

        def block(a, b):
            return table[a * vectors : (a + 1) * vectors, b * vectors : (b + 1) * vectors]

        gram = block(0, 0) + (block(0, 1) + block(1, 0)) + (block(1, 1) + (block(0, 2) + block(2, 0)))
        gram_ref[...] = gram * scale


def finish_kernel(gram_ref, filtered_ref, out_ref, upper_ref, inverse_ref):
    vectors = gram_ref.shape[0]

    @pl.when(pl.program_id(0) == 0)
    def _():
        rows = lax.broadcasted_iota(jnp.int32, (vectors, vectors), 0)
        cols = lax.broadcasted_iota(jnp.int32, (vectors, vectors), 1)
        rest = gram_ref[...]
        inverse = (rows == cols).astype(jnp.float32)
        factor = jnp.zeros_like(rest)
        for k in range(vectors):
            root = lax.rsqrt(rest[k : k + 1, k : k + 1])
            top = rest[k : k + 1, :] * root
            column = rest[:, k : k + 1] * root
            below = jnp.where(rows[:, :1] > k, column, 0.0)
            inverse_row = inverse[k : k + 1, :] * root
            factor = jnp.where(rows == k, jnp.where(cols >= k, top, 0.0), factor)
            inverse = jnp.where(rows == k, inverse_row, inverse - below * inverse_row)
            rest = rest - below * top
        upper_ref[...] = factor
        inverse_ref[...] = inverse

    left = pieces(inverse_ref[...], 3)
    right = pieces(filtered_ref[...], 3)
    order = ((0, 0), (0, 1), (1, 0), (1, 1), (0, 2), (2, 0))
    out_ref[...] = jnp.dot(
        jnp.concatenate([left[a] for a, _ in order], axis=1),
        jnp.concatenate([right[b] for _, b in order], axis=0),
        preferred_element_type=jnp.float32,
    )


def local(previous, current, field_levels, bond_levels, lo_bits):
    vectors, amp_count = current.shape
    site_count = field_levels.shape[0]
    devices = lax.axis_size("hi") * lax.axis_size("lo")
    local_bits = amp_count.bit_length() - 1
    global_bits = devices.bit_length() - 1
    rest_bits = local_bits - global_bits
    device = lax.axis_index("hi") * lax.axis_size("lo") + lax.axis_index("lo")
    local_index = lax.iota(jnp.int32, amp_count)
    scale = 4.0 / site_count

    def position(site_number):
        if site_number < global_bits:
            return rest_bits + site_number
        return site_number - global_bits

    def device_bit(k):
        return device >> k & 1

    def spin_value(site_number):
        if site_number < local_bits:
            return 0.5 - (local_index >> position(site_number) & 1).astype(jnp.float32)
        return 0.5 - device_bit(site_number - local_bits).astype(jnp.float32)

    def permute(values, pairs):
        return lax.ppermute(values, AXES, pairs)

    def flips(mask, keep=lambda i: True):
        return [(i, i ^ mask) for i in range(devices) if keep(i)]

    fields = FIELD_STEP * field_levels.astype(jnp.float32)
    couplings = COUPLING_STEP * bond_levels.astype(jnp.float32)
    strength = scale * (0.5 * couplings)

    triples = []
    swaps = {}
    for m in range(1, global_bits - 1, 2):
        sum_low = m == 1
        first, second, site = triple_pairs(devices, m - 1, m, m + 1, sum_low)
        triples.append((m, first, second, site, m + 1 if sum_low else m - 1))
    firsts = [permute(current, first) for _, first, _, _, _ in triples]
    for _, _, _, _, bit in triples:
        if bit not in swaps:
            swaps[bit] = permute(current, flips(1 << bit))
    extra = []
    if global_bits % 2 == 0:
        top = global_bits - 1
        moved = permute(current, [(i, i ^ (3 << top - 1)) for i in range(devices) if (i >> top & 1) != (i >> top - 1 & 1)])
        extra.append(strength[site_count - 2] * moved)

    span = 2 ** (rest_bits - 1)
    tiled = span >= LANES
    side = 1 - device_bit(0)
    if tiled:
        half = take_half(current, side.reshape(1), span)
    else:
        half = lax.dynamic_index_in_dim(current.reshape(vectors, -1, 2, span), side, 2, False).reshape(vectors, -1)
    middle = (1, 2) if global_bits > 1 else (0, 1)
    mask = 3 if global_bits > 1 else 1
    half_early = permute(half, flips(1, lambda i: (i & mask) in middle))

    diagonal = jnp.zeros((amp_count,), jnp.float32)
    for site_number in range(site_count):
        diagonal = diagonal + fields[site_number] * spin_value(site_number)
        if site_number < site_count - 1:
            diagonal = diagonal + couplings[site_number] * spin_value(site_number) * spin_value(site_number + 1)
    rows = lax.iota(jnp.int32, GROUP)[:, None]
    cols = lax.iota(jnp.int32, GROUP)[None, :]
    matrix = jnp.zeros((GROUP, GROUP), jnp.float32)
    tile_bonds, tile_weights, wraps, wrap_weights = [], [], [], []
    for site_number in range(local_bits - 1):
        one, two = position(site_number), position(site_number + 1)
        low, high = min(one, two), max(one, two)
        if high < GROUP_BITS:
            differ = (cols >> low & 1) != (cols >> high & 1)
            target = rows == cols ^ (1 << low | 1 << high)
            matrix = matrix + jnp.where(differ & target, 0.5 * couplings[site_number], 0.0)
        elif low >= LANE_BITS:
            tile_bonds.append((low - LANE_BITS, high - LANE_BITS))
            tile_weights.append(strength[site_number])
        else:
            wraps.append((high - LANE_BITS, low))
            wrap_weights.append(strength[site_number])
    weights = jnp.stack(tile_weights + wrap_weights + [jnp.float32(scale)])
    here = pl.pallas_call(
        functools.partial(local_kernel, tile_bonds=tuple(tile_bonds), wraps=tuple(wraps)),
        out_shape=jax.ShapeDtypeStruct((vectors, amp_count), jnp.float32),
        in_specs=[smem()] + [pl.BlockSpec(memory_space=pltpu.VMEM)] * 4,
        out_specs=pl.BlockSpec(memory_space=pltpu.VMEM),
        compiler_params=params(),
        name="local_bonds",
    )(weights, current, previous, (scale * diagonal)[None, :], matrix.astype(jnp.bfloat16))

    seconds = []
    own = []
    for (m, _, second, site, bit), arrived in zip(triples, firsts):
        low_strength = strength[local_bits + m - 1]
        high_strength = strength[local_bits + m]
        at_site = functools.reduce(
            jnp.logical_and, [device_bit(m - 1 + j) == (site[j] ^ device_bit(m) ^ site[1]) for j in range(3)]
        )
        sent = jnp.where(at_site, low_strength, 0.0) * swaps[bit] + high_strength * arrived
        seconds.append(permute(sent, second))
        uses = (device_bit(m - 1) != device_bit(m)) & (device_bit(m + 1) == device_bit(m))
        own.append(jnp.where(uses, low_strength, 0.0))
    late = half
    if firsts:
        late, _ = lax.optimization_barrier((half, firsts[0]))
    half_late = permute(late, flips(1, lambda i: (i & mask) not in middle))
    half_strength = strength[local_bits - 1]
    half_weights = [jnp.where(side == 0, half_strength, 0.0), jnp.where(side == 1, half_strength, 0.0)]

    while len(own) < 2:
        own.append(jnp.float32(0.0))
        firsts.append(current)
        seconds.append(jnp.zeros_like(current))
    for arrived, weight, more in zip(firsts[2:], own[2:], seconds[2:]):
        extra.append(weight * arrived + more)
    if not tiled:
        both = half_strength * (half_early + half_late)
        placed = jnp.where(lax.iota(jnp.int32, 2)[None, None, :, None] == side, both.reshape(vectors, -1, 1, span), 0.0)
        extra.append(placed.reshape(vectors, amp_count))
        half_early = half_late = jnp.zeros_like(half)
        span = LANES
    for term in extra:
        here = here + term
    steps = 4
    block = pl.BlockSpec((vectors, amp_count // steps), lambda i: (0, i))
    half_block = pl.BlockSpec((vectors, amp_count // 2 // steps), lambda i: (0, i))
    weights = jnp.stack(own[:2] + half_weights)
    acc = pl.pallas_call(
        functools.partial(gather_kernel, span=span),
        grid=(steps,),
        out_shape=jax.ShapeDtypeStruct((vectors, amp_count), jnp.float32),
        in_specs=[smem(), block, block, block, half_block],
        out_specs=block,
        compiler_params=params(),
        name="gather_first",
    )(weights, here, firsts[0], firsts[1], half_early)
    filtered, gram = pl.pallas_call(
        functools.partial(filter_kernel, span=span, scale=1.0 / (amp_count * devices)),
        grid=(steps,),
        out_shape=(
            jax.ShapeDtypeStruct((vectors, amp_count), jnp.float32),
            jax.ShapeDtypeStruct((vectors, vectors), jnp.float32),
        ),
        in_specs=[smem(), block, block, block, half_block],
        out_specs=(block, pl.BlockSpec((vectors, vectors), lambda i: (0, 0))),
        scratch_shapes=[pltpu.VMEM((3 * vectors, 3 * vectors), jnp.float32)],
        compiler_params=params(),
        name="filter_gram",
    )(weights, acc, seconds[0], seconds[1], half_late)

    hub = lo_bits
    gram = gram + permute(gram, flips(1 << hub, lambda i: not i >> hub & 1))
    for k in range(global_bits):
        if k != hub:
            gram = gram + permute(gram, flips(1 << k, lambda i: i >> hub & 1))
    gram = jnp.where(device_bit(hub) == 1, gram, permute(gram, flips(1 << hub, lambda i: i >> hub & 1)))

    return pl.pallas_call(
        finish_kernel,
        grid=(steps,),
        out_shape=(
            jax.ShapeDtypeStruct((vectors, amp_count), jnp.float32),
            jax.ShapeDtypeStruct((vectors, vectors), jnp.float32),
        ),
        in_specs=[pl.BlockSpec((vectors, vectors), lambda i: (0, 0)), block],
        out_specs=(block, pl.BlockSpec((vectors, vectors), lambda i: (0, 0))),
        scratch_shapes=[pltpu.VMEM((vectors, vectors), jnp.float32)],
        compiler_params=params(),
        name="factor_apply",
    )(gram, filtered)


def solution(mesh):
    in_specs = (P(None, AXES), P(None, AXES), P(), P())
    out_specs = (P(None, AXES), P())
    lo_bits = mesh.shape["lo"].bit_length() - 1
    return jax.shard_map(
        functools.partial(local, lo_bits=lo_bits), mesh=mesh, in_specs=in_specs, out_specs=out_specs, check_vma=False
    )
```

```python
import functools

import jax
import jax.numpy as jnp
from jax import lax
from jax.experimental import pallas as pl
from jax.experimental.pallas import tpu as pltpu
from jax.sharding import PartitionSpec as P

FIELD_STEP = 0.75
COUPLING_STEP = 0.5
AXES = ("hi", "lo")
LANES = 128
LANE_BITS = 7
GROUP = 256
GROUP_BITS = 8
VMEM_LIMIT = 48 * 1024 * 1024


def pieces(values, count):
    parts = []
    for _ in range(count):
        part = values.astype(jnp.bfloat16)
        parts.append(part)
        values = values - part.astype(jnp.float32)
    return parts


def smem():
    return pl.BlockSpec(memory_space=pltpu.SMEM)


def params():
    return pltpu.CompilerParams(vmem_limit_bytes=VMEM_LIMIT)


FIRST = {(0, 1, 0): (1, 0, 0), (1, 1, 0): (0, 1, 0), (1, 0, 0): (0, 0, 0), (0, 0, 0): (0, 0, 1)}
SECOND = {(0, 1, 0): (1, 0, 1), (1, 0, 0): (0, 0, 1), (0, 0, 0): (1, 0, 0), (1, 1, 0): (1, 1, 1)}
BOTH = {(0, 1, 0): (1, 0, 0), (1, 0, 0): (0, 1, 0), (1, 1, 0): (1, 1, 1), (0, 0, 0): (0, 0, 1)}
ON = {(1, 0, 1): (1, 1, 1), (0, 0, 0): (0, 1, 0), (1, 0, 0): (0, 0, 1), (0, 0, 1): (1, 0, 0)}


def route(devices, m, table):
    full = {}
    for one, two in table.items():
        full[one] = two
        full[tuple(1 - b for b in one)] = tuple(1 - b for b in two)
    pairs = []
    for device in range(devices):
        goal = full[tuple(device >> m + j & 1 for j in (-1, 0, 1))]
        pairs.append((device, device & ~(7 << m - 1) | goal[0] << m - 1 | goal[1] << m | goal[2] << m + 1))
    return pairs


def bit_of(device_ref, k):
    return device_ref[0] >> k & 1


def cost(flops, moved):
    return pl.CostEstimate(flops=flops, bytes_accessed=moved, transcendentals=0)


def strength_of(bond_ref, bond, scale):
    return bond_ref[bond].astype(jnp.float32) * (0.5 * COUPLING_STEP * scale)


def tile_of(ref, t):
    return ref[:, t * LANES : (t + 1) * LANES]


def across(ref, t, bit):
    if bit >= LANE_BITS:
        return tile_of(ref, t ^ (1 << bit - LANE_BITS))
    values = tile_of(ref, t)
    lane = lax.broadcasted_iota(jnp.int32, values.shape, 1)
    return jnp.where(lane >> bit & 1 == 1, pltpu.roll(values, 1 << bit, 1), pltpu.roll(values, LANES - (1 << bit), 1))


def sided(pair, t, bit):
    if bit >= LANE_BITS:
        return pair[t >> bit - LANE_BITS & 1]
    lane = lax.broadcasted_iota(jnp.int32, (1, LANES), 1)
    return jnp.where(lane >> bit & 1 == 1, pair[1], pair[0])


def local_kernel(device_ref, field_ref, bond_ref, x_ref, prev_ref, out_ref, *, global_bits, scale):
    vectors, amp_count = x_ref.shape
    local_bits = amp_count.bit_length() - 1
    rest_bits = local_bits - global_bits
    site_count = field_ref.shape[0]
    tile_bits = local_bits - LANE_BITS

    def position(site):
        if site >= local_bits:
            return site
        return rest_bits + site if site < global_bits else site - global_bits

    fields = [field_ref[s].astype(jnp.float32) * (FIELD_STEP * scale) for s in range(site_count)]
    couplings = [bond_ref[s].astype(jnp.float32) * COUPLING_STEP for s in range(site_count - 1)]
    scaled = [value * scale for value in couplings]
    lane = lax.broadcasted_iota(jnp.int32, (1, LANES), 1)
    lane_spin = [0.5 - (lane >> k & 1).astype(jnp.float32) for k in range(LANE_BITS)]
    far_spin = [0.5 - bit_of(device_ref, k).astype(jnp.float32) for k in range(site_count - local_bits)]

    lane_row = jnp.zeros((1, LANES), jnp.float32)
    rest = jnp.float32(0.0)
    fields_of = [jnp.float32(0.0)] * tile_bits
    bonds_of = [[] for _ in range(tile_bits)]
    mixed = []
    for s in range(site_count):
        spot = position(s)
        if spot < LANE_BITS:
            lane_row = lane_row + fields[s] * lane_spin[spot]
        elif spot < local_bits:
            fields_of[spot - LANE_BITS] = fields_of[spot - LANE_BITS] + fields[s]
        else:
            rest = rest + fields[s] * far_spin[spot - local_bits]
        if s == site_count - 1:
            continue
        low, high = sorted((spot, position(s + 1)))
        if high < LANE_BITS:
            lane_row = lane_row + scaled[s] * (lane_spin[low] * lane_spin[high])
        elif high < local_bits and low >= LANE_BITS:
            bonds_of[high - LANE_BITS].append((low - LANE_BITS, scaled[s]))
        elif high < local_bits:
            mixed.append((high - LANE_BITS, scaled[s] * lane_spin[low]))
        elif low >= local_bits:
            rest = rest + scaled[s] * (far_spin[low - local_bits] * far_spin[high - local_bits])
        elif low >= LANE_BITS:
            fields_of[low - LANE_BITS] = fields_of[low - LANE_BITS] + scaled[s] * far_spin[high - local_bits]
        else:
            lane_row = lane_row + scaled[s] * far_spin[high - local_bits] * lane_spin[low]
    number = [rest]
    for k in range(tile_bits):
        longer = []
        for up in (0, 1):
            for t, value in enumerate(number):
                term = (0.5 - up) * fields_of[k]
                for other, coupling in bonds_of[k]:
                    term = term + (0.5 - up) * (0.5 - (t >> other & 1)) * coupling
                longer.append(value + term)
        number = longer
    mixed_bits = sorted({bit for bit, _ in mixed})
    lane_rows = {}
    for pattern in range(1 << len(mixed_bits)):
        row = lane_row
        for bit, vector in mixed:
            row = row + (0.5 - (pattern >> mixed_bits.index(bit) & 1)) * vector
        lane_rows[pattern] = row

    rows = lax.broadcasted_iota(jnp.int32, (GROUP, GROUP), 0)
    cols = lax.broadcasted_iota(jnp.int32, (GROUP, GROUP), 1)
    change = rows ^ cols
    matrix = jnp.zeros((GROUP, GROUP), jnp.float32)
    tile_bonds, wraps = [], []
    for s in range(local_bits - 1):
        low, high = sorted((position(s), position(s + 1)))
        if high < GROUP_BITS:
            chosen = (change == (1 << low | 1 << high)) & ((cols >> low & 1) != (cols >> high & 1))
            matrix = jnp.where(chosen, 0.5 * couplings[s], matrix)
        elif low >= LANE_BITS:
            tile_bonds.append((low - LANE_BITS, high - LANE_BITS, 0.5 * scaled[s]))
        else:
            shown = [jnp.where((lane >> low & 1) != up, 0.5 * scaled[s], 0.0) for up in (0, 1)]
            wraps.append((high - LANE_BITS, low, shown))
    matrix = matrix.astype(jnp.bfloat16)
    stacked = jnp.concatenate([x_ref[:, k * GROUP : (k + 1) * GROUP] for k in range(amp_count // GROUP)], axis=0)
    product = None
    for part in pieces(stacked, 3):
        term = jnp.dot(part, matrix, preferred_element_type=jnp.float32)
        product = term if product is None else product + term

    def tile(t):
        return x_ref[:, t * LANES : (t + 1) * LANES]

    for t in range(amp_count // LANES):
        row = t // 2 * vectors
        side = (t & 1) * LANES
        pattern = sum((t >> bit & 1) << j for j, bit in enumerate(mixed_bits))
        total = (lane_rows[pattern] + number[t]) * tile(t) - prev_ref[:, t * LANES : (t + 1) * LANES]
        total = total + scale * product[row : row + vectors, side : side + LANES]
        for one, two, weight in tile_bonds:
            if (t >> one & 1) != (t >> two & 1):
                total = total + weight * tile(t ^ (1 << one) ^ (1 << two))
        for high, low, shown in wraps:
            up = t >> high & 1
            shift = 1 << low if up == 0 else LANES - (1 << low)
            total = total + shown[up] * pltpu.roll(tile(t ^ (1 << high)), shift, 1)
        out_ref[:, t * LANES : (t + 1) * LANES] = total


def sent_kernel(device_ref, bond_ref, own_ref, swap_ref, arrived_ref, out_ref, *, bit, bond, scale):
    p, m, q = (bit_of(device_ref, k) for k in range(3))
    joint, low, high = (strength_of(bond_ref, bond + k, scale) for k in range(3))
    at_sum = (p != m) & (q != m)
    passing = (p != m) & (q == m)
    corner = (p == m) & (q == m)
    low = jnp.where(at_sum, low, 0.0)
    high = jnp.where(p != m, high, 0.0)
    swap_pair = [jnp.where(passing & (p == side), joint, 0.0) for side in (0, 1)]
    own_pair = [jnp.where(corner & (p == side), joint, 0.0) for side in (0, 1)]
    for t in range(out_ref.shape[1] // LANES):
        total = low * tile_of(swap_ref, t) + high * tile_of(arrived_ref, t)
        total = total + sided(swap_pair, t, bit) * across(swap_ref, t, bit)
        total = total + sided(own_pair, t, bit) * across(own_ref, t, bit)
        out_ref[:, t * LANES : (t + 1) * LANES] = total


def gather_kernel(device_ref, bond_ref, local_ref, first_ref, *refs, bit, local_bits, scale):
    out_ref = refs[-1]
    p, m, q = (bit_of(device_ref, k) for k in range(3))
    joint, low = (strength_of(bond_ref, local_bits - 1 + k, scale) for k in range(2))
    low = jnp.where((p != m) & (q == m), low, 0.0)
    halves = ((p == m) & (q == m)) | ((p != m) & (q != m))
    pair = [jnp.where(halves & (p != side), joint, 0.0) for side in (0, 1)]
    weights = []
    for k in range(len(refs) - 1):
        differ = bit_of(device_ref, 2 * k + 2) != bit_of(device_ref, 2 * k + 3)
        weights.append(jnp.where(differ, strength_of(bond_ref, local_bits + 2 * k + 2, scale), 0.0))
    for t in range(out_ref.shape[1] // LANES):
        total = tile_of(local_ref, t) + low * tile_of(first_ref, t)
        total = total + sided(pair, t, bit) * across(first_ref, t, bit)
        for weight, ref in zip(weights, refs):
            total = total + weight * tile_of(ref, t)
        out_ref[:, t * LANES : (t + 1) * LANES] = total


def packed(gram, vectors):
    fold = max(1, LANES // vectors)
    rows = vectors // fold
    return jnp.concatenate([gram[k * rows : (k + 1) * rows, :] for k in range(fold)], axis=1)


def unpacked(table, vectors):
    fold = max(1, LANES // vectors)
    return jnp.concatenate([table[:, k * vectors : (k + 1) * vectors] for k in range(fold)], axis=0)


def filter_kernel(device_ref, bond_ref, acc_ref, second_ref, *refs, local_bits, scale, share):
    out_ref, gram_ref, total_ref = refs[-3:]
    step = pl.program_id(0)
    vectors = acc_ref.shape[0]
    weights = []
    for k in range(len(refs) - 3):
        differ = bit_of(device_ref, 2 * k + 3) != bit_of(device_ref, 2 * k + 4)
        weights.append(jnp.where(differ, strength_of(bond_ref, local_bits + 2 * k + 3, scale), 0.0))

    @pl.when(step == 0)
    def _():
        total_ref[...] = jnp.zeros_like(total_ref)

    total = acc_ref[...] + second_ref[...]
    for weight, ref in zip(weights, refs):
        total = total + weight * ref[...]
    out_ref[...] = total
    stacked = jnp.concatenate(pieces(out_ref[...], 3), axis=0)
    total_ref[...] += lax.dot_general(
        stacked, stacked, (((1,), (1,)), ((), ())), preferred_element_type=jnp.float32
    )

    @pl.when(step == pl.num_programs(0) - 1)
    def _():
        table = total_ref[...]

        def block(a, b):
            return table[a * vectors : (a + 1) * vectors, b * vectors : (b + 1) * vectors]

        gram = block(0, 0) + (block(0, 1) + block(1, 0)) + (block(1, 1) + (block(0, 2) + block(2, 0)))
        gram_ref[...] = packed(gram * share, vectors)


def finish_kernel(gram_ref, filtered_ref, out_ref, upper_ref, inverse_ref):
    vectors = filtered_ref.shape[0]

    @pl.when(pl.program_id(0) == 0)
    def _():
        rows = lax.broadcasted_iota(jnp.int32, (vectors, vectors), 0)
        cols = lax.broadcasted_iota(jnp.int32, (vectors, vectors), 1)
        rest = unpacked(gram_ref[...], vectors)
        inverse = (rows == cols).astype(jnp.float32)
        factor = jnp.zeros_like(rest)
        for k in range(vectors):
            root = lax.rsqrt(rest[k : k + 1, k : k + 1])
            top = rest[k : k + 1, :] * root
            column = rest[:, k : k + 1] * root
            below = jnp.where(rows[:, :1] > k, column, 0.0)
            inverse_row = inverse[k : k + 1, :] * root
            factor = jnp.where(rows == k, jnp.where(cols >= k, top, 0.0), factor)
            inverse = jnp.where(rows == k, inverse_row, inverse - below * inverse_row)
            rest = rest - below * top
        upper_ref[...] = factor
        inverse_ref[...] = inverse

    left = pieces(inverse_ref[...], 3)
    right = pieces(filtered_ref[...], 3)
    order = ((0, 0), (0, 1), (1, 0), (1, 1), (0, 2), (2, 0))
    out_ref[...] = jnp.dot(
        jnp.concatenate([left[a] for a, _ in order], axis=1),
        jnp.concatenate([right[b] for _, b in order], axis=0),
        preferred_element_type=jnp.float32,
    )


def local(previous, current, field_levels, bond_levels, lo_bits):
    vectors, amp_count = current.shape
    site_count = field_levels.shape[0]
    devices = lax.axis_size("hi") * lax.axis_size("lo")
    local_bits = amp_count.bit_length() - 1
    global_bits = devices.bit_length() - 1
    rest_bits = local_bits - global_bits
    device = lax.axis_index("hi") * lax.axis_size("lo") + lax.axis_index("lo")
    place = device.astype(jnp.int32).reshape(1)
    scale = 4.0 / site_count
    whole = jax.ShapeDtypeStruct((vectors, amp_count), jnp.float32)
    size = vectors * amp_count
    steps = 4
    block = pl.BlockSpec((vectors, amp_count // steps), lambda i: (0, i))
    vmem = pl.BlockSpec(memory_space=pltpu.VMEM)

    def permute(values, pairs):
        return lax.ppermute(values, AXES, pairs)

    def flips(mask, keep=lambda i: True):
        return [(i, i ^ mask) for i in range(devices) if keep(i)]

    def strength(bond):
        return (scale * 0.5 * COUPLING_STEP) * bond_levels[bond].astype(jnp.float32)

    middles = tuple(range(3, global_bits - 1, 2))
    first = permute(current, route(devices, 1, FIRST))
    swap = permute(current, flips(4))
    boths = [permute(current, route(devices, m, BOTH)) for m in middles]
    extra = []
    if global_bits % 2 == 0:
        top = global_bits - 1
        moved = permute(current, flips(3 << top - 1, lambda i: (i >> top & 1) != (i >> top - 1 & 1)))
        extra.append(strength(site_count - 2) * moved)

    here = pl.pallas_call(
        functools.partial(local_kernel, global_bits=global_bits, scale=scale),
        out_shape=whole,
        in_specs=[smem()] * 3 + [vmem] * 2,
        out_specs=vmem,
        compiler_params=params(),
        cost_estimate=cost(6 * size * GROUP, 12 * size),
        name="local_bonds",
    )(place, field_levels, bond_levels, current, previous)
    first, here = lax.optimization_barrier((first, here))

    sent = pl.pallas_call(
        functools.partial(sent_kernel, bit=rest_bits - 1, bond=local_bits - 1, scale=scale),
        grid=(steps,),
        out_shape=whole,
        in_specs=[smem()] * 2 + [block] * 3,
        out_specs=block,
        compiler_params=params(),
        cost_estimate=cost(6 * size, 16 * size),
        name="sent_on",
    )(place, bond_levels, current, swap, first)
    second = permute(sent, route(devices, 1, SECOND))
    ons = [permute(both, route(devices, m, ON)) for m, both in zip(middles, boths)]

    for term in extra:
        here = here + term
    acc = pl.pallas_call(
        functools.partial(gather_kernel, bit=rest_bits - 1, local_bits=local_bits, scale=scale),
        grid=(steps,),
        out_shape=whole,
        in_specs=[smem()] * 2 + [block] * (2 + len(boths)),
        out_specs=block,
        compiler_params=params(),
        cost_estimate=cost(6 * size, 16 * size),
        name="gather_first",
    )(place, bond_levels, here, first, *boths)
    fold = max(1, LANES // vectors)
    table = (vectors // fold, vectors * fold)
    table_block = pl.BlockSpec(table, lambda i: (0, 0))
    filtered, gram = pl.pallas_call(
        functools.partial(filter_kernel, local_bits=local_bits, scale=scale, share=1.0 / (amp_count * devices)),
        grid=(steps,),
        out_shape=(whole, jax.ShapeDtypeStruct(table, jnp.float32)),
        in_specs=[smem()] * 2 + [block] * (2 + len(ons)),
        out_specs=(block, table_block),
        scratch_shapes=[pltpu.VMEM((3 * vectors, 3 * vectors), jnp.float32)],
        compiler_params=params(),
        cost_estimate=cost(6 * size * vectors, 16 * size),
        name="filter_gram",
    )(place, bond_levels, acc, second, *ons)

    for k in [lo_bits] + [k for k in range(global_bits) if k != lo_bits]:
        gram = gram + permute(gram, flips(1 << k))

    return pl.pallas_call(
        finish_kernel,
        grid=(steps,),
        out_shape=(whole, jax.ShapeDtypeStruct((vectors, vectors), jnp.float32)),
        in_specs=[table_block, block],
        out_specs=(block, pl.BlockSpec((vectors, vectors), lambda i: (0, 0))),
        scratch_shapes=[pltpu.VMEM((vectors, vectors), jnp.float32)],
        compiler_params=params(),
        cost_estimate=cost(12 * size * vectors, 8 * size),
        name="factor_apply",
    )(gram, filtered)


def solution(mesh):
    in_specs = (P(None, AXES), P(None, AXES), P(), P())
    out_specs = (P(None, AXES), P())
    lo_bits = mesh.shape["lo"].bit_length() - 1
    return jax.shard_map(
        functools.partial(local, lo_bits=lo_bits), mesh=mesh, in_specs=in_specs, out_specs=out_specs, check_vma=False
    )
```

```python
import functools

import jax
import jax.numpy as jnp
from jax import lax
from jax.experimental import pallas as pl
from jax.experimental.pallas import tpu as pltpu
from jax.sharding import PartitionSpec as P

FIELD_STEP = 0.75
COUPLING_STEP = 0.5
AXES = ("hi", "lo")
LANES = 128
SUBLANES = 8
LANE_BITS = 7
GROUP = 256
CHUNK = 1024
OUT_CHUNK = 2048
GROUP_BITS = 8
VMEM_LIMIT = 48 * 1024 * 1024


def pieces(values, count):
    parts = []
    for _ in range(count):
        part = values.astype(jnp.bfloat16)
        parts.append(part)
        values = values - part.astype(jnp.float32)
    return parts


def smem():
    return pl.BlockSpec(memory_space=pltpu.SMEM)


def params(limit=VMEM_LIMIT):
    return pltpu.CompilerParams(vmem_limit_bytes=limit)


FIRST = {(0, 1, 0): (1, 0, 0), (1, 1, 0): (0, 1, 0), (1, 0, 0): (0, 0, 0), (0, 0, 0): (0, 0, 1)}
SECOND = {(0, 1, 0): (1, 0, 1), (1, 0, 0): (0, 0, 1), (0, 0, 0): (1, 0, 0), (1, 1, 0): (1, 1, 1)}
BOTH = {(0, 1, 0): (1, 0, 0), (1, 0, 0): (0, 1, 0), (1, 1, 0): (1, 1, 1), (0, 0, 0): (0, 0, 1)}
ON = {(1, 0, 1): (1, 1, 1), (0, 0, 0): (0, 1, 0), (1, 0, 0): (0, 0, 1), (0, 0, 1): (1, 0, 0)}


def route(devices, m, table):
    full = {}
    for one, two in table.items():
        full[one] = two
        full[tuple(1 - b for b in one)] = tuple(1 - b for b in two)
    pairs = []
    for device in range(devices):
        goal = full[tuple(device >> m + j & 1 for j in (-1, 0, 1))]
        pairs.append((device, device & ~(7 << m - 1) | goal[0] << m - 1 | goal[1] << m | goal[2] << m + 1))
    return pairs


def bit_of(device_ref, k):
    return device_ref[0] >> k & 1


def cost(flops, moved):
    return pl.CostEstimate(flops=flops, bytes_accessed=moved, transcendentals=0)


def strength_of(bond_ref, bond, scale):
    return bond_ref[bond].astype(jnp.float32) * (0.5 * COUPLING_STEP * scale)


def tile_of(ref, t):
    return ref[:, t * LANES : (t + 1) * LANES]


def across(ref, t, bit):
    if bit >= LANE_BITS:
        return tile_of(ref, t ^ (1 << bit - LANE_BITS))
    values = tile_of(ref, t)
    lane = lax.broadcasted_iota(jnp.int32, values.shape, 1)
    return jnp.where(lane >> bit & 1 == 1, pltpu.roll(values, 1 << bit, 1), pltpu.roll(values, LANES - (1 << bit), 1))


def sided(pair, t, bit):
    if bit >= LANE_BITS:
        return pair[t >> bit - LANE_BITS & 1]
    lane = lax.broadcasted_iota(jnp.int32, (1, LANES), 1)
    return jnp.where(lane >> bit & 1 == 1, pair[1], pair[0])


def local_kernel(device_ref, field_ref, bond_ref, x_ref, prev_ref, out_ref, *, global_bits, scale):
    vectors, amp_count = x_ref.shape
    local_bits = amp_count.bit_length() - 1
    rest_bits = local_bits - global_bits
    site_count = field_ref.shape[0]
    tile_bits = local_bits - LANE_BITS

    def position(site):
        if site >= local_bits:
            return site
        return rest_bits + site if site < global_bits else site - global_bits

    fields = [field_ref[s].astype(jnp.float32) * (FIELD_STEP * scale) for s in range(site_count)]
    couplings = [bond_ref[s].astype(jnp.float32) * COUPLING_STEP for s in range(site_count - 1)]
    scaled = [value * scale for value in couplings]
    lane = lax.broadcasted_iota(jnp.int32, (1, LANES), 1)
    lane_spin = [0.5 - (lane >> k & 1).astype(jnp.float32) for k in range(LANE_BITS)]
    far_spin = [0.5 - bit_of(device_ref, k).astype(jnp.float32) for k in range(site_count - local_bits)]

    lane_row = jnp.zeros((1, LANES), jnp.float32)
    rest = jnp.float32(0.0)
    fields_of = [jnp.float32(0.0)] * tile_bits
    bonds_of = [[] for _ in range(tile_bits)]
    mixed = []
    for s in range(site_count):
        spot = position(s)
        if spot < LANE_BITS:
            lane_row = lane_row + fields[s] * lane_spin[spot]
        elif spot < local_bits:
            fields_of[spot - LANE_BITS] = fields_of[spot - LANE_BITS] + fields[s]
        else:
            rest = rest + fields[s] * far_spin[spot - local_bits]
        if s == site_count - 1:
            continue
        low, high = sorted((spot, position(s + 1)))
        if high < LANE_BITS:
            lane_row = lane_row + scaled[s] * (lane_spin[low] * lane_spin[high])
        elif high < local_bits and low >= LANE_BITS:
            bonds_of[high - LANE_BITS].append((low - LANE_BITS, scaled[s]))
        elif high < local_bits:
            mixed.append((high - LANE_BITS, scaled[s] * lane_spin[low]))
        elif low >= local_bits:
            rest = rest + scaled[s] * (far_spin[low - local_bits] * far_spin[high - local_bits])
        elif low >= LANE_BITS:
            fields_of[low - LANE_BITS] = fields_of[low - LANE_BITS] + scaled[s] * far_spin[high - local_bits]
        else:
            lane_row = lane_row + scaled[s] * far_spin[high - local_bits] * lane_spin[low]
    number = [rest]
    for k in range(tile_bits):
        longer = []
        for up in (0, 1):
            for t, value in enumerate(number):
                term = (0.5 - up) * fields_of[k]
                for other, coupling in bonds_of[k]:
                    term = term + (0.5 - up) * (0.5 - (t >> other & 1)) * coupling
                longer.append(value + term)
        number = longer
    mixed_bits = sorted({bit for bit, _ in mixed})
    lane_rows = {}
    for pattern in range(1 << len(mixed_bits)):
        row = lane_row
        for bit, vector in mixed:
            row = row + (0.5 - (pattern >> mixed_bits.index(bit) & 1)) * vector
        lane_rows[pattern] = row

    rows = lax.broadcasted_iota(jnp.int32, (GROUP, GROUP), 0)
    cols = lax.broadcasted_iota(jnp.int32, (GROUP, GROUP), 1)
    change = rows ^ cols
    matrix = jnp.zeros((GROUP, GROUP), jnp.float32)
    tile_bonds, wraps = [], []
    for s in range(local_bits - 1):
        low, high = sorted((position(s), position(s + 1)))
        if high < GROUP_BITS:
            chosen = (change == (1 << low | 1 << high)) & ((cols >> low & 1) != (cols >> high & 1))
            matrix = jnp.where(chosen, 0.5 * couplings[s], matrix)
        elif low >= LANE_BITS:
            tile_bonds.append((low - LANE_BITS, high - LANE_BITS, 0.5 * scaled[s]))
        else:
            shown = [jnp.where((lane >> low & 1) != up, 0.5 * scaled[s], 0.0) for up in (0, 1)]
            wraps.append((high - LANE_BITS, low, shown))
    matrix = matrix.astype(jnp.bfloat16)
    stacked = jnp.concatenate([x_ref[:, k * GROUP : (k + 1) * GROUP] for k in range(amp_count // GROUP)], axis=0)
    product = None
    for part in pieces(stacked, 3):
        term = jnp.dot(part, matrix, preferred_element_type=jnp.float32)
        product = term if product is None else product + term

    def tile(t):
        return x_ref[:, t * LANES : (t + 1) * LANES]

    for t in range(amp_count // LANES):
        row = t // 2 * vectors
        side = (t & 1) * LANES
        pattern = sum((t >> bit & 1) << j for j, bit in enumerate(mixed_bits))
        total = (lane_rows[pattern] + number[t]) * tile(t) - prev_ref[:, t * LANES : (t + 1) * LANES]
        total = total + scale * product[row : row + vectors, side : side + LANES]
        for one, two, weight in tile_bonds:
            if (t >> one & 1) != (t >> two & 1):
                total = total + weight * tile(t ^ (1 << one) ^ (1 << two))
        for high, low, shown in wraps:
            up = t >> high & 1
            shift = 1 << low if up == 0 else LANES - (1 << low)
            total = total + shown[up] * pltpu.roll(tile(t ^ (1 << high)), shift, 1)
        out_ref[:, t * LANES : (t + 1) * LANES] = total


def cut_kernel(x_ref, out_ref, held_ref, in_sems, out_sems, *, start):
    rows, width = held_ref.shape
    strips = [pl.ds(k * SUBLANES, SUBLANES) for k in range(rows // SUBLANES)]
    loads = [
        pltpu.make_async_copy(x_ref.at[strip, pl.ds(start, width)], held_ref.at[strip], in_sems.at[k])
        for k, strip in enumerate(strips)
    ]
    stores = [
        pltpu.make_async_copy(held_ref.at[strip], out_ref.at[strip], out_sems.at[k]) for k, strip in enumerate(strips)
    ]
    for load in loads:
        load.start()
    for load, store in zip(loads, stores):
        load.wait()
        store.start()
    for store in stores:
        store.wait()


def cut(values, start, width):
    rows = values.shape[0]
    hbm = pl.BlockSpec(memory_space=pltpu.HBM)
    strips = rows // SUBLANES
    return pl.pallas_call(
        functools.partial(cut_kernel, start=start),
        out_shape=jax.ShapeDtypeStruct((rows, width), values.dtype),
        in_specs=[hbm],
        out_specs=hbm,
        scratch_shapes=[
            pltpu.VMEM((rows, width), values.dtype),
            pltpu.SemaphoreType.DMA((strips,)),
            pltpu.SemaphoreType.DMA((strips,)),
        ],
        compiler_params=params(63 * 1024 * 1024),
        cost_estimate=cost(0, 8 * rows * width),
        name=f"cut_{start}",
    )(values)


def sent_kernel(device_ref, bond_ref, own_ref, swap_ref, arrived_ref, out_ref, *, start, bit, bond, scale):
    p, m, q = (bit_of(device_ref, k) for k in range(3))
    joint, low, high = (strength_of(bond_ref, bond + k, scale) for k in range(3))
    at_sum = (p != m) & (q != m)
    passing = (p != m) & (q == m)
    corner = (p == m) & (q == m)
    low = jnp.where(at_sum, low, 0.0)
    high = jnp.where(p != m, high, 0.0)
    swap_pair = [jnp.where(passing & (p == side), joint, 0.0) for side in (0, 1)]
    own_pair = [jnp.where(corner & (p == side), joint, 0.0) for side in (0, 1)]
    for t in range(out_ref.shape[1] // LANES):
        total = low * tile_of(swap_ref, start + t) + high * tile_of(arrived_ref, t)
        total = total + sided(swap_pair, t, bit) * across(swap_ref, start + t, bit)
        total = total + sided(own_pair, t, bit) * across(own_ref, start + t, bit)
        out_ref[:, t * LANES : (t + 1) * LANES] = total


def gather_kernel(device_ref, bond_ref, local_ref, first_ref, *refs, start, bit, local_bits, scale):
    out_ref = refs[-1]
    p, m, q = (bit_of(device_ref, k) for k in range(3))
    joint, low = (strength_of(bond_ref, local_bits - 1 + k, scale) for k in range(2))
    low = jnp.where((p != m) & (q == m), low, 0.0)
    halves = ((p == m) & (q == m)) | ((p != m) & (q != m))
    pair = [jnp.where(halves & (p != side), joint, 0.0) for side in (0, 1)]
    weights = []
    for k in range(len(refs) - 1):
        differ = bit_of(device_ref, 2 * k + 2) != bit_of(device_ref, 2 * k + 3)
        weights.append(jnp.where(differ, strength_of(bond_ref, local_bits + 2 * k + 2, scale), 0.0))
    for t in range(out_ref.shape[1] // LANES):
        total = tile_of(local_ref, start + t) + low * tile_of(first_ref, t)
        total = total + sided(pair, t, bit) * across(first_ref, t, bit)
        for weight, ref in zip(weights, refs):
            total = total + weight * tile_of(ref, t)
        out_ref[:, t * LANES : (t + 1) * LANES] = total


def packed(gram, vectors):
    fold = max(1, LANES // vectors)
    rows = vectors // fold
    return jnp.concatenate([gram[k * rows : (k + 1) * rows, :] for k in range(fold)], axis=1)


def unpacked(table, vectors):
    fold = max(1, LANES // vectors)
    return jnp.concatenate([table[:, k * vectors : (k + 1) * vectors] for k in range(fold)], axis=0)


def filter_kernel(device_ref, bond_ref, before_ref, acc_ref, second_ref, *refs, local_bits, scale, share, last):
    out_ref, gram_ref = refs[-2:]
    vectors, amp_count = acc_ref.shape
    weights = []
    for k in range(len(refs) - 2):
        differ = bit_of(device_ref, 2 * k + 3) != bit_of(device_ref, 2 * k + 4)
        weights.append(jnp.where(differ, strength_of(bond_ref, local_bits + 2 * k + 3, scale), 0.0))
    table = before_ref[...]
    for first in range(0, amp_count, CHUNK):
        cols = slice(first, min(first + CHUNK, amp_count))
        total = acc_ref[:, cols] + second_ref[:, cols]
        for weight, ref in zip(weights, refs):
            total = total + weight * ref[:, cols]
        out_ref[:, cols] = total
        stacked = jnp.concatenate(pieces(total, 3), axis=0)
        table = table + lax.dot_general(
            stacked, stacked, (((1,), (1,)), ((), ())), preferred_element_type=jnp.float32
        )
    if not last:
        gram_ref[...] = table
        return

    def block(a, b):
        return table[a * vectors : (a + 1) * vectors, b * vectors : (b + 1) * vectors]

    gram = block(0, 0) + (block(0, 1) + block(1, 0)) + (block(1, 1) + (block(0, 2) + block(2, 0)))
    gram_ref[...] = packed(gram * share, vectors)


def reciprocal(values):
    guess = pl.reciprocal(values, approx=True)
    guess = guess * (2.0 - values * guess)
    return guess * (2.0 - values * guess)


def factor(gram):
    vectors = gram.shape[0]
    lanes = max(LANES, 2 * vectors)
    rows = lax.broadcasted_iota(jnp.int32, (vectors, lanes), 0)
    cols = lax.broadcasted_iota(jnp.int32, (vectors, lanes), 1)
    rest = jnp.concatenate([gram, jnp.zeros((vectors, lanes - vectors), jnp.float32)], axis=1)
    rest = rest + (cols == rows + vectors).astype(jnp.float32)
    for i in range(0, vectors, 2):
        j = i + 1
        left = jnp.broadcast_to(rest[:, i:j], rest.shape)
        right = jnp.broadcast_to(rest[:, j : j + 1], rest.shape)
        one, two = rest[i:j, :], rest[j : j + 1, :]
        a, b, d = left[i:j, :], left[j : j + 1, :], right[j : j + 1, :]
        scale = reciprocal(a * d - b * b)
        update = left * ((d * one - b * two) * scale) + right * ((a * two - b * one) * scale)
        rest = rest - jnp.where(rows > j, update, 0.0)
    diagonal = jnp.sum(jnp.where(cols == rows, rest, 0.0), axis=1, keepdims=True)
    odd = (rows & 1) == 1
    corner = jnp.sum(jnp.where((cols == rows - 1) & odd, rest, 0.0), axis=1, keepdims=True)
    before = pltpu.roll(rest, 1, 0)
    lead = pltpu.roll(jnp.broadcast_to(diagonal, rest.shape), 1, 0)
    ratio = jnp.where(odd, corner * reciprocal(lead), 0.0)
    rest = (rest - ratio * before) * lax.rsqrt(diagonal - corner * ratio)
    return jnp.where(cols >= rows, rest, 0.0)[:, :vectors], rest[:, vectors : 2 * vectors]


def finish_kernel(gram_ref, *refs):
    out_ref, upper_ref, held_ref, sems = refs[-4:]
    vectors = out_ref.shape[0]
    upper, inverse = factor(unpacked(gram_ref[...], vectors))
    upper_ref[...] = upper
    high, middle, low = pieces(inverse, 3)
    none = jnp.zeros_like(high)
    left = jnp.concatenate(
        [
            jnp.concatenate([high, high, high], axis=1),
            jnp.concatenate([middle, middle, none], axis=1),
            jnp.concatenate([low, none, none], axis=1),
        ],
        axis=0,
    )
    copies = []
    place = 0
    for ref in refs[:-4]:
        for first in range(0, ref.shape[1], OUT_CHUNK):
            count = min(OUT_CHUNK, ref.shape[1] - first)
            right = jnp.concatenate(pieces(ref[:, first : first + count], 3), axis=0)
            product = jnp.dot(left, right, preferred_element_type=jnp.float32)
            held_ref[:, place : place + count] = product[:vectors] + (
                product[vectors : 2 * vectors] + product[2 * vectors :]
            )
            cols = pl.ds(place, count)
            copies.append(
                pltpu.make_async_copy(held_ref.at[:, cols], out_ref.at[:, cols], sems.at[len(copies)])
            )
            copies[-1].start()
            place += count
    for copy in copies:
        copy.wait()


def local(previous, current, field_levels, bond_levels, lo_bits):
    vectors, amp_count = current.shape
    site_count = field_levels.shape[0]
    devices = lax.axis_size("hi") * lax.axis_size("lo")
    local_bits = amp_count.bit_length() - 1
    global_bits = devices.bit_length() - 1
    rest_bits = local_bits - global_bits
    device = lax.axis_index("hi") * lax.axis_size("lo") + lax.axis_index("lo")
    place = device.astype(jnp.int32).reshape(1)
    scale = 4.0 / site_count
    whole = jax.ShapeDtypeStruct((vectors, amp_count), jnp.float32)
    size = vectors * amp_count
    vmem = pl.BlockSpec(memory_space=pltpu.VMEM)

    def permute(values, pairs):
        return lax.ppermute(values, AXES, pairs)

    def flips(mask, keep=lambda i: True):
        return [(i, i ^ mask) for i in range(devices) if keep(i)]

    def strength(bond):
        return (scale * 0.5 * COUPLING_STEP) * bond_levels[bond].astype(jnp.float32)

    middles = tuple(range(3, global_bits - 1, 2))
    width = amp_count // 4
    parts = [(0, 2), (2, 2)]
    swap = permute(current, flips(4))
    firsts, boths = [], []
    for start, count in parts:
        piece = cut(current, start * width, count * width)
        firsts.append(permute(piece, route(devices, 1, FIRST)))
        boths.append([permute(piece, route(devices, m, BOTH)) for m in middles])

    here = pl.pallas_call(
        functools.partial(local_kernel, global_bits=global_bits, scale=scale),
        out_shape=whole,
        in_specs=[smem()] * 3 + [vmem] * 2,
        out_specs=vmem,
        compiler_params=params(),
        cost_estimate=cost(6 * size * GROUP, 12 * size),
        name="local_bonds",
    )(place, field_levels, bond_levels, current, previous)
    firsts[0], here = lax.optimization_barrier((firsts[0], here))
    if global_bits % 2 == 0:
        top = global_bits - 1
        moved = permute(current, flips(3 << top - 1, lambda i: (i >> top & 1) != (i >> top - 1 & 1)))
        here = here + strength(site_count - 2) * moved

    seconds, ons, accs = [], [], []
    for (start, count), first, both in zip(parts, firsts, boths):
        shape = jax.ShapeDtypeStruct((vectors, count * width), jnp.float32)
        part_size = vectors * count * width
        if accs:
            first, _ = lax.optimization_barrier((first, accs[-1]))
        sent = pl.pallas_call(
            functools.partial(
                sent_kernel, start=start * width // LANES, bit=rest_bits - 1, bond=local_bits - 1, scale=scale
            ),
            out_shape=shape,
            in_specs=[smem()] * 2 + [vmem] * 3,
            out_specs=vmem,
            compiler_params=params(),
            cost_estimate=cost(0, 0),
            name=f"sent_on_{start}",
        )(place, bond_levels, current, swap, first)
        seconds.append(permute(sent, route(devices, 1, SECOND)))
        both, sent = lax.optimization_barrier((both, sent))
        ons.append([permute(values, route(devices, m, ON)) for m, values in zip(middles, both)])
        accs.append(
            pl.pallas_call(
                functools.partial(
                    gather_kernel, start=start * width // LANES, bit=rest_bits - 1, local_bits=local_bits, scale=scale
                ),
                out_shape=shape,
                in_specs=[smem()] * 2 + [vmem] * (2 + len(both)),
                out_specs=vmem,
                compiler_params=params(),
                cost_estimate=cost(0, 0),
                name=f"gather_first_{start}",
            )(place, bond_levels, here, first, *both)
        )

    fold = max(1, LANES // vectors)
    table = (vectors // fold, vectors * fold)
    square = (3 * vectors, 3 * vectors)
    filtered = []
    products = jnp.zeros(square, jnp.float32)
    for number, ((start, count), acc, second, on) in enumerate(zip(parts, accs, seconds, ons)):
        last = number == len(parts) - 1
        part_size = vectors * count * width
        done, products = pl.pallas_call(
            functools.partial(
                filter_kernel, local_bits=local_bits, scale=scale, share=1.0 / (amp_count * devices), last=last
            ),
            out_shape=(
                jax.ShapeDtypeStruct((vectors, count * width), jnp.float32),
                jax.ShapeDtypeStruct(table if last else square, jnp.float32),
            ),
            in_specs=[smem()] * 2 + [vmem] * (3 + len(on)),
            out_specs=(vmem, vmem),
            compiler_params=params(),
            cost_estimate=cost(6 * part_size * vectors, 16 * part_size),
            name=f"filter_gram_{start}",
        )(place, bond_levels, products, acc, second, *on)
        filtered.append(done)
    gram = products

    hub = 1 << lo_bits
    gram = gram + permute(gram, flips(hub))
    for k in [k for k in range(global_bits) if k > lo_bits] + list(range(lo_bits)):
        gram = gram + permute(gram, flips(1 << k | hub))

    chunks = sum(-(-values.shape[1] // OUT_CHUNK) for values in filtered)
    return pl.pallas_call(
        finish_kernel,
        out_shape=(whole, jax.ShapeDtypeStruct((vectors, vectors), jnp.float32)),
        in_specs=[vmem] * (1 + len(filtered)),
        out_specs=(pl.BlockSpec(memory_space=pltpu.HBM), vmem),
        scratch_shapes=[pltpu.VMEM((vectors, amp_count), jnp.float32), pltpu.SemaphoreType.DMA((chunks,))],
        compiler_params=params(),
        cost_estimate=cost(12 * size * vectors, 8 * size),
        name="factor_apply",
    )(gram, *filtered)


def solution(mesh):
    in_specs = (P(None, AXES), P(None, AXES), P(), P())
    out_specs = (P(None, AXES), P())
    lo_bits = mesh.shape["lo"].bit_length() - 1
    return jax.shard_map(
        functools.partial(local, lo_bits=lo_bits), mesh=mesh, in_specs=in_specs, out_specs=out_specs, check_vma=False
    )
```

```python
import functools

import jax
import jax.numpy as jnp
from jax import lax
from jax.experimental import pallas as pl
from jax.experimental.pallas import tpu as pltpu
from jax.sharding import PartitionSpec as P

FIELD_STEP = 0.75
COUPLING_STEP = 0.5
AXES = ("hi", "lo")
LANES = 128
SUBLANES = 8
LANE_BITS = 7
GROUP = 256
CHUNK = 1024
OUT_CHUNK = 2048
PANEL = 16
GROUP_BITS = 8
VMEM_LIMIT = 48 * 1024 * 1024
CUT_LIMIT = 56 * 1024 * 1024


def pieces(values, count):
    parts = []
    for _ in range(count):
        part = values.astype(jnp.bfloat16)
        parts.append(part)
        values = values - part.astype(jnp.float32)
    return parts


def smem():
    return pl.BlockSpec(memory_space=pltpu.SMEM)


def params(limit=VMEM_LIMIT):
    return pltpu.CompilerParams(vmem_limit_bytes=limit)


FIRST = {(0, 1, 0): (1, 0, 0), (1, 1, 0): (0, 1, 0), (1, 0, 0): (0, 0, 0), (0, 0, 0): (0, 0, 1)}
SECOND = {(0, 1, 0): (1, 0, 1), (1, 0, 0): (0, 0, 1), (0, 0, 0): (1, 0, 0), (1, 1, 0): (1, 1, 1)}
BOTH = {(0, 1, 0): (1, 0, 0), (1, 0, 0): (0, 1, 0), (1, 1, 0): (1, 1, 1), (0, 0, 0): (0, 0, 1)}
ON = {(1, 0, 1): (1, 1, 1), (0, 0, 0): (0, 1, 0), (1, 0, 0): (0, 0, 1), (0, 0, 1): (1, 0, 0)}


def route(devices, m, table):
    full = {}
    for one, two in table.items():
        full[one] = two
        full[tuple(1 - b for b in one)] = tuple(1 - b for b in two)
    pairs = []
    for device in range(devices):
        goal = full[tuple(device >> m + j & 1 for j in (-1, 0, 1))]
        pairs.append((device, device & ~(7 << m - 1) | goal[0] << m - 1 | goal[1] << m | goal[2] << m + 1))
    return pairs


def bit_of(device_ref, k):
    return device_ref[0] >> k & 1


def cost(flops, moved):
    return pl.CostEstimate(flops=flops, bytes_accessed=moved, transcendentals=0)


def strength_of(bond_ref, bond, scale):
    return bond_ref[bond].astype(jnp.float32) * (0.5 * COUPLING_STEP * scale)


def tile_of(ref, t):
    return ref[:, t * LANES : (t + 1) * LANES]


def across(ref, t, bit):
    if bit >= LANE_BITS:
        return tile_of(ref, t ^ (1 << bit - LANE_BITS))
    values = tile_of(ref, t)
    lane = lax.broadcasted_iota(jnp.int32, values.shape, 1)
    return jnp.where(lane >> bit & 1 == 1, pltpu.roll(values, 1 << bit, 1), pltpu.roll(values, LANES - (1 << bit), 1))


def sided(pair, t, bit):
    if bit >= LANE_BITS:
        return pair[t >> bit - LANE_BITS & 1]
    lane = lax.broadcasted_iota(jnp.int32, (1, LANES), 1)
    return jnp.where(lane >> bit & 1 == 1, pair[1], pair[0])


def local_kernel(device_ref, field_ref, bond_ref, x_ref, prev_ref, out_ref, *, global_bits, scale):
    vectors, amp_count = x_ref.shape
    local_bits = amp_count.bit_length() - 1
    rest_bits = local_bits - global_bits
    site_count = field_ref.shape[0]
    tile_bits = local_bits - LANE_BITS

    def position(site):
        if site >= local_bits:
            return site
        return rest_bits + site if site < global_bits else site - global_bits

    fields = [field_ref[s].astype(jnp.float32) * (FIELD_STEP * scale) for s in range(site_count)]
    couplings = [bond_ref[s].astype(jnp.float32) * COUPLING_STEP for s in range(site_count - 1)]
    scaled = [value * scale for value in couplings]
    lane = lax.broadcasted_iota(jnp.int32, (1, LANES), 1)
    lane_spin = [0.5 - (lane >> k & 1).astype(jnp.float32) for k in range(LANE_BITS)]
    far_spin = [0.5 - bit_of(device_ref, k).astype(jnp.float32) for k in range(site_count - local_bits)]

    lane_row = jnp.zeros((1, LANES), jnp.float32)
    rest = jnp.float32(0.0)
    fields_of = [jnp.float32(0.0)] * tile_bits
    bonds_of = [[] for _ in range(tile_bits)]
    mixed = []
    for s in range(site_count):
        spot = position(s)
        if spot < LANE_BITS:
            lane_row = lane_row + fields[s] * lane_spin[spot]
        elif spot < local_bits:
            fields_of[spot - LANE_BITS] = fields_of[spot - LANE_BITS] + fields[s]
        else:
            rest = rest + fields[s] * far_spin[spot - local_bits]
        if s == site_count - 1:
            continue
        low, high = sorted((spot, position(s + 1)))
        if high < LANE_BITS:
            lane_row = lane_row + scaled[s] * (lane_spin[low] * lane_spin[high])
        elif high < local_bits and low >= LANE_BITS:
            bonds_of[high - LANE_BITS].append((low - LANE_BITS, scaled[s]))
        elif high < local_bits:
            mixed.append((high - LANE_BITS, scaled[s] * lane_spin[low]))
        elif low >= local_bits:
            rest = rest + scaled[s] * (far_spin[low - local_bits] * far_spin[high - local_bits])
        elif low >= LANE_BITS:
            fields_of[low - LANE_BITS] = fields_of[low - LANE_BITS] + scaled[s] * far_spin[high - local_bits]
        else:
            lane_row = lane_row + scaled[s] * far_spin[high - local_bits] * lane_spin[low]
    number = [rest]
    for k in range(tile_bits):
        longer = []
        for up in (0, 1):
            for t, value in enumerate(number):
                term = (0.5 - up) * fields_of[k]
                for other, coupling in bonds_of[k]:
                    term = term + (0.5 - up) * (0.5 - (t >> other & 1)) * coupling
                longer.append(value + term)
        number = longer
    mixed_bits = sorted({bit for bit, _ in mixed})
    lane_rows = {}
    for pattern in range(1 << len(mixed_bits)):
        row = lane_row
        for bit, vector in mixed:
            row = row + (0.5 - (pattern >> mixed_bits.index(bit) & 1)) * vector
        lane_rows[pattern] = row

    rows = lax.broadcasted_iota(jnp.int32, (GROUP, GROUP), 0)
    cols = lax.broadcasted_iota(jnp.int32, (GROUP, GROUP), 1)
    change = rows ^ cols
    matrix = jnp.zeros((GROUP, GROUP), jnp.float32)
    tile_bonds, wraps = [], []
    for s in range(local_bits - 1):
        low, high = sorted((position(s), position(s + 1)))
        if high < GROUP_BITS:
            chosen = (change == (1 << low | 1 << high)) & ((cols >> low & 1) != (cols >> high & 1))
            matrix = jnp.where(chosen, 0.5 * couplings[s], matrix)
        elif low >= LANE_BITS:
            tile_bonds.append((low - LANE_BITS, high - LANE_BITS, 0.5 * scaled[s]))
        else:
            shown = [jnp.where((lane >> low & 1) != up, 0.5 * scaled[s], 0.0) for up in (0, 1)]
            wraps.append((high - LANE_BITS, low, shown))
    matrix = matrix.astype(jnp.bfloat16)
    stacked = jnp.concatenate([x_ref[:, k * GROUP : (k + 1) * GROUP] for k in range(amp_count // GROUP)], axis=0)
    product = None
    for part in pieces(stacked, 3):
        term = jnp.dot(part, matrix, preferred_element_type=jnp.float32)
        product = term if product is None else product + term

    def tile(t):
        return x_ref[:, t * LANES : (t + 1) * LANES]

    for t in range(amp_count // LANES):
        row = t // 2 * vectors
        side = (t & 1) * LANES
        pattern = sum((t >> bit & 1) << j for j, bit in enumerate(mixed_bits))
        total = (lane_rows[pattern] + number[t]) * tile(t) - prev_ref[:, t * LANES : (t + 1) * LANES]
        total = total + scale * product[row : row + vectors, side : side + LANES]
        for one, two, weight in tile_bonds:
            if (t >> one & 1) != (t >> two & 1):
                total = total + weight * tile(t ^ (1 << one) ^ (1 << two))
        for high, low, shown in wraps:
            up = t >> high & 1
            shift = 1 << low if up == 0 else LANES - (1 << low)
            total = total + shown[up] * pltpu.roll(tile(t ^ (1 << high)), shift, 1)
        out_ref[:, t * LANES : (t + 1) * LANES] = total


def cut_kernel(x_ref, out_ref, sems, *, start):
    rows, width = out_ref.shape
    copies = []
    for k in range(rows // SUBLANES):
        strip = pl.ds(k * SUBLANES, SUBLANES)
        copies.append(
            pltpu.make_async_copy(x_ref.at[strip, pl.ds(start, width)], out_ref.at[strip], sems.at[k])
        )
        copies[-1].start()
    for copy in copies:
        copy.wait()


def cut(values, start, width):
    rows = values.shape[0]
    return pl.pallas_call(
        functools.partial(cut_kernel, start=start),
        out_shape=jax.ShapeDtypeStruct((rows, width), values.dtype),
        in_specs=[pl.BlockSpec(memory_space=pltpu.HBM)],
        out_specs=pl.BlockSpec(memory_space=pltpu.VMEM),
        scratch_shapes=[pltpu.SemaphoreType.DMA((rows // SUBLANES,))],
        compiler_params=params(CUT_LIMIT),
        cost_estimate=cost(0, 8 * rows * width),
        name=f"cut_{start}",
    )(values)


def ready_kernel(device_ref, bond_ref, own_ref, swap_ref, *out_refs, bit, bond, scale):
    p, m, q = (bit_of(device_ref, k) for k in range(3))
    joint, low = (strength_of(bond_ref, bond + k, scale) for k in range(2))
    low = jnp.where((p != m) & (q != m), low, 0.0)
    passing = (p != m) & (q == m)
    corner = (p == m) & (q == m)
    swap_pair = [jnp.where(passing & (p == side), joint, 0.0) for side in (0, 1)]
    own_pair = [jnp.where(corner & (p == side), joint, 0.0) for side in (0, 1)]
    t = 0
    for out_ref in out_refs:
        for place in range(out_ref.shape[1] // LANES):
            total = low * tile_of(swap_ref, t) + sided(swap_pair, t, bit) * across(swap_ref, t, bit)
            total = total + sided(own_pair, t, bit) * across(own_ref, t, bit)
            out_ref[:, place * LANES : (place + 1) * LANES] = total
            t += 1


def sent_kernel(device_ref, bond_ref, ready_ref, arrived_ref, out_ref, *, bond, scale):
    high = strength_of(bond_ref, bond + 2, scale)
    high = jnp.where(bit_of(device_ref, 0) != bit_of(device_ref, 1), high, 0.0)
    out_ref[...] = ready_ref[...] + high * arrived_ref[...]


def gather_kernel(device_ref, bond_ref, local_ref, first_ref, *refs, start, bit, local_bits, scale):
    out_ref = refs[-1]
    p, m, q = (bit_of(device_ref, k) for k in range(3))
    joint, low = (strength_of(bond_ref, local_bits - 1 + k, scale) for k in range(2))
    low = jnp.where((p != m) & (q == m), low, 0.0)
    halves = ((p == m) & (q == m)) | ((p != m) & (q != m))
    pair = [jnp.where(halves & (p != side), joint, 0.0) for side in (0, 1)]
    weights = []
    for k in range(len(refs) - 1):
        differ = bit_of(device_ref, 2 * k + 2) != bit_of(device_ref, 2 * k + 3)
        weights.append(jnp.where(differ, strength_of(bond_ref, local_bits + 2 * k + 2, scale), 0.0))
    for t in range(out_ref.shape[1] // LANES):
        total = tile_of(local_ref, start + t) + low * tile_of(first_ref, t)
        total = total + sided(pair, t, bit) * across(first_ref, t, bit)
        for weight, ref in zip(weights, refs):
            total = total + weight * tile_of(ref, t)
        out_ref[:, t * LANES : (t + 1) * LANES] = total


def packed(gram, vectors):
    fold = max(1, LANES // vectors)
    rows = vectors // fold
    return jnp.concatenate([gram[k * rows : (k + 1) * rows, :] for k in range(fold)], axis=1)


def unpacked(table, vectors):
    fold = max(1, LANES // vectors)
    return jnp.concatenate([table[:, k * vectors : (k + 1) * vectors] for k in range(fold)], axis=0)


def filter_kernel(device_ref, bond_ref, before_ref, acc_ref, second_ref, *refs, local_bits, scale, share, last):
    out_ref, gram_ref = refs[-2:]
    vectors, amp_count = acc_ref.shape
    weights = []
    for k in range(len(refs) - 2):
        differ = bit_of(device_ref, 2 * k + 3) != bit_of(device_ref, 2 * k + 4)
        weights.append(jnp.where(differ, strength_of(bond_ref, local_bits + 2 * k + 3, scale), 0.0))
    table = before_ref[...]
    for first in range(0, amp_count, CHUNK):
        cols = slice(first, min(first + CHUNK, amp_count))
        total = acc_ref[:, cols] + second_ref[:, cols]
        for weight, ref in zip(weights, refs):
            total = total + weight * ref[:, cols]
        out_ref[:, cols] = total
        stacked = jnp.concatenate(pieces(total, 3), axis=0)
        table = table + lax.dot_general(
            stacked, stacked, (((1,), (1,)), ((), ())), preferred_element_type=jnp.float32
        )
    if not last:
        gram_ref[...] = table
        return

    def block(a, b):
        return table[a * vectors : (a + 1) * vectors, b * vectors : (b + 1) * vectors]

    gram = block(0, 0) + (block(0, 1) + block(1, 0)) + (block(1, 1) + (block(0, 2) + block(2, 0)))
    gram_ref[...] = packed(gram * share, vectors)


def reciprocal(values):
    guess = pl.reciprocal(values, approx=True)
    return guess * (2.0 - values * guess)


def factor(gram):
    vectors = gram.shape[0]
    lanes = max(LANES, 2 * vectors)
    rows = lax.broadcasted_iota(jnp.int32, (vectors, lanes), 0)
    cols = lax.broadcasted_iota(jnp.int32, (vectors, lanes), 1)
    rest = jnp.concatenate([gram, jnp.zeros((vectors, lanes - vectors), jnp.float32)], axis=1)
    rest = rest + (cols == rows + vectors).astype(jnp.float32)
    for panel in range(0, vectors, PANEL):
        columns = [jnp.broadcast_to(rest[:, k : k + 1], rest.shape) for k in range(panel, min(panel + PANEL, vectors))]
        for k in range(0, len(columns), 2):
            i, j = panel + k, panel + k + 1
            left, right = columns[k : k + 2]
            a, b, d = left[i:j, :], left[j : j + 1, :], right[j : j + 1, :]
            scale = reciprocal(a * d - b * b)
            left = jnp.where(rows > j, left, 0.0)
            right = jnp.where(rows > j, right, 0.0)

            def eliminate(values):
                one, two = values[i:j, :], values[j : j + 1, :]
                return values - (left * ((d * one - b * two) * scale) + right * ((a * two - b * one) * scale))

            columns[k + 2 :] = [eliminate(values) for values in columns[k + 2 :]]
            rest = eliminate(rest)
    diagonal = jnp.sum(jnp.where(cols == rows, rest, 0.0), axis=1, keepdims=True)
    odd = (rows & 1) == 1
    corner = jnp.sum(jnp.where((cols == rows - 1) & odd, rest, 0.0), axis=1, keepdims=True)
    before = pltpu.roll(rest, 1, 0)
    lead = pltpu.roll(jnp.broadcast_to(diagonal, rest.shape), 1, 0)
    ratio = jnp.where(odd, corner * reciprocal(lead), 0.0)
    rest = (rest - ratio * before) * lax.rsqrt(diagonal - corner * ratio)
    return jnp.where(cols >= rows, rest, 0.0)[:, :vectors], rest[:, vectors : 2 * vectors]


def finish_kernel(gram_ref, *refs):
    out_ref, upper_ref, held_ref, sems = refs[-4:]
    vectors = out_ref.shape[0]
    upper, inverse = factor(unpacked(gram_ref[...], vectors))
    upper_ref[...] = upper
    high, middle, low = pieces(inverse, 3)
    none = jnp.zeros_like(high)
    left = jnp.concatenate(
        [
            jnp.concatenate([high, high, high, low], axis=1),
            jnp.concatenate([middle, middle, none, none], axis=1),
        ],
        axis=0,
    )
    copies = []
    place = 0
    for ref in refs[:-4]:
        for first in range(0, ref.shape[1], OUT_CHUNK):
            count = min(OUT_CHUNK, ref.shape[1] - first)
            right = pieces(ref[:, first : first + count], 3)
            product = jnp.dot(left, jnp.concatenate(right + right[:1], axis=0), preferred_element_type=jnp.float32)
            held_ref[:, place : place + count] = product[:vectors] + product[vectors:]
            cols = pl.ds(place, count)
            copies.append(
                pltpu.make_async_copy(held_ref.at[:, cols], out_ref.at[:, cols], sems.at[len(copies)])
            )
            copies[-1].start()
            place += count
    for copy in copies:
        copy.wait()


def local(previous, current, field_levels, bond_levels, lo_bits):
    vectors, amp_count = current.shape
    site_count = field_levels.shape[0]
    devices = lax.axis_size("hi") * lax.axis_size("lo")
    local_bits = amp_count.bit_length() - 1
    global_bits = devices.bit_length() - 1
    rest_bits = local_bits - global_bits
    device = lax.axis_index("hi") * lax.axis_size("lo") + lax.axis_index("lo")
    place = device.astype(jnp.int32).reshape(1)
    scale = 4.0 / site_count
    whole = jax.ShapeDtypeStruct((vectors, amp_count), jnp.float32)
    size = vectors * amp_count
    vmem = pl.BlockSpec(memory_space=pltpu.VMEM)

    def permute(values, pairs):
        return lax.ppermute(values, AXES, pairs)

    def flips(mask, keep=lambda i: True):
        return [(i, i ^ mask) for i in range(devices) if keep(i)]

    def strength(bond):
        return (scale * 0.5 * COUPLING_STEP) * bond_levels[bond].astype(jnp.float32)

    middles = tuple(range(3, global_bits - 1, 2))
    width = amp_count // 32
    parts = [(0, 20), (20, 12)]
    swap = permute(current, flips(4))
    firsts, boths = [], []
    for start, count in parts:
        piece = cut(current, start * width, count * width)
        firsts.append(permute(piece, route(devices, 1, FIRST)))
        boths.append([permute(piece, route(devices, m, BOTH)) for m in middles])

    current, _ = lax.optimization_barrier((current, piece))

    here = pl.pallas_call(
        functools.partial(local_kernel, global_bits=global_bits, scale=scale),
        out_shape=whole,
        in_specs=[smem()] * 3 + [vmem] * 2,
        out_specs=vmem,
        compiler_params=params(),
        cost_estimate=cost(6 * size * GROUP, 12 * size),
        name="local_bonds",
    )(place, field_levels, bond_levels, current, previous)
    ready = pl.pallas_call(
        functools.partial(ready_kernel, bit=rest_bits - 1, bond=local_bits - 1, scale=scale),
        out_shape=tuple(jax.ShapeDtypeStruct((vectors, count * width), jnp.float32) for _, count in parts),
        in_specs=[smem()] * 2 + [vmem] * 2,
        out_specs=tuple(vmem for _ in parts),
        compiler_params=params(),
        cost_estimate=cost(6 * size, 12 * size),
        name="ready",
    )(place, bond_levels, current, swap)
    firsts[0], here, ready = lax.optimization_barrier((firsts[0], here, ready))
    if global_bits % 2 == 0:
        top = global_bits - 1
        moved = permute(current, flips(3 << top - 1, lambda i: (i >> top & 1) != (i >> top - 1 & 1)))
        here = here + strength(site_count - 2) * moved

    seconds, ons, accs, sents = [], [], [], []
    for (start, count), first, both, base in zip(parts, firsts, boths, ready):
        shape = jax.ShapeDtypeStruct((vectors, count * width), jnp.float32)
        part_size = vectors * count * width
        sent = pl.pallas_call(
            functools.partial(sent_kernel, bond=local_bits - 1, scale=scale),
            out_shape=shape,
            in_specs=[smem()] * 2 + [vmem] * 2,
            out_specs=vmem,
            compiler_params=params(),
            cost_estimate=cost(0, 0),
            name=f"sent_on_{start}",
        )(place, bond_levels, base, first)
        seconds.append(permute(sent, route(devices, 1, SECOND)))
        sents.append(sent)
        both, sent = lax.optimization_barrier((both, sent))
        ons.append([permute(values, route(devices, m, ON)) for m, values in zip(middles, both)])
    firsts, sents = lax.optimization_barrier((firsts, sents))
    for (start, count), first, both in zip(parts, firsts, boths):
        shape = jax.ShapeDtypeStruct((vectors, count * width), jnp.float32)
        part_size = vectors * count * width
        accs.append(
            pl.pallas_call(
                functools.partial(
                    gather_kernel, start=start * width // LANES, bit=rest_bits - 1, local_bits=local_bits, scale=scale
                ),
                out_shape=shape,
                in_specs=[smem()] * 2 + [vmem] * (2 + len(both)),
                out_specs=vmem,
                compiler_params=params(),
                cost_estimate=cost(0, 0),
                name=f"gather_first_{start}",
            )(place, bond_levels, here, first, *both)
        )

    fold = max(1, LANES // vectors)
    table = (vectors // fold, vectors * fold)
    square = (3 * vectors, 3 * vectors)
    filtered = []
    products = jnp.zeros(square, jnp.float32)
    for number, ((start, count), acc, second, on) in enumerate(zip(parts, accs, seconds, ons)):
        last = number == len(parts) - 1
        part_size = vectors * count * width
        done, products = pl.pallas_call(
            functools.partial(
                filter_kernel, local_bits=local_bits, scale=scale, share=1.0 / (amp_count * devices), last=last
            ),
            out_shape=(
                jax.ShapeDtypeStruct((vectors, count * width), jnp.float32),
                jax.ShapeDtypeStruct(table if last else square, jnp.float32),
            ),
            in_specs=[smem()] * 2 + [vmem] * (3 + len(on)),
            out_specs=(vmem, vmem),
            compiler_params=params(),
            cost_estimate=cost(6 * part_size * vectors, 16 * part_size),
            name=f"filter_gram_{start}",
        )(place, bond_levels, products, acc, second, *on)
        filtered.append(done)
    gram = products

    hub = 1 << lo_bits
    gram = gram + permute(gram, flips(hub))
    for k in [k for k in range(global_bits) if k > lo_bits] + list(range(lo_bits)):
        gram = gram + permute(gram, flips(1 << k | hub))

    chunks = sum(-(-values.shape[1] // OUT_CHUNK) for values in filtered)
    return pl.pallas_call(
        finish_kernel,
        out_shape=(whole, jax.ShapeDtypeStruct((vectors, vectors), jnp.float32)),
        in_specs=[vmem] * (1 + len(filtered)),
        out_specs=(pl.BlockSpec(memory_space=pltpu.HBM), vmem),
        scratch_shapes=[pltpu.VMEM((vectors, amp_count), jnp.float32), pltpu.SemaphoreType.DMA((chunks,))],
        compiler_params=params(),
        cost_estimate=cost(12 * size * vectors, 8 * size),
        name="factor_apply",
    )(gram, *filtered)


def solution(mesh):
    in_specs = (P(None, AXES), P(None, AXES), P(), P())
    out_specs = (P(None, AXES), P())
    lo_bits = mesh.shape["lo"].bit_length() - 1
    return jax.shard_map(
        functools.partial(local, lo_bits=lo_bits), mesh=mesh, in_specs=in_specs, out_specs=out_specs, check_vma=False
    )
```

```python
import functools

import jax
import jax.numpy as jnp
from jax import lax
from jax.experimental import pallas as pl
from jax.experimental.pallas import tpu as pltpu
from jax.sharding import PartitionSpec as P

FIELD_STEP = 0.75
COUPLING_STEP = 0.5
AXES = ("hi", "lo")
LANES = 128
SUBLANES = 8
LANE_BITS = 7
GROUP = 256
CHUNK = 1024
OUT_CHUNK = 2048
PANEL = 16
GROUP_BITS = 8
VMEM_LIMIT = 28 * 1024 * 1024
ADD_COST = 10**9
CUT_LIMIT = 56 * 1024 * 1024


def pieces(values, count):
    parts = []
    for _ in range(count):
        part = values.astype(jnp.bfloat16)
        parts.append(part)
        values = values - part.astype(jnp.float32)
    return parts


def smem():
    return pl.BlockSpec(memory_space=pltpu.SMEM)


def params(limit=VMEM_LIMIT):
    return pltpu.CompilerParams(vmem_limit_bytes=limit)


FIRST = {(0, 1, 0): (1, 0, 0), (1, 1, 0): (0, 1, 0), (1, 0, 0): (0, 0, 0), (0, 0, 0): (0, 0, 1)}
SECOND = {(0, 1, 0): (1, 0, 1), (1, 0, 0): (0, 0, 1), (0, 0, 0): (1, 0, 0), (1, 1, 0): (1, 1, 1)}
LATER_FIRST = {(0, 1, 0): (1, 0, 0), (1, 1, 0): (1, 1, 1)}
LATER_SECOND = {(1, 1, 1): (1, 0, 1), (1, 0, 0): (0, 0, 1)}


def route(devices, m, table):
    full = {}
    for one, two in table.items():
        full[one] = two
        full[tuple(1 - b for b in one)] = tuple(1 - b for b in two)
    pairs = []
    for device in range(devices):
        goal = full.get(tuple(device >> m + j & 1 for j in (-1, 0, 1)))
        if goal is None:
            continue
        pairs.append((device, device & ~(7 << m - 1) | goal[0] << m - 1 | goal[1] << m | goal[2] << m + 1))
    return pairs


def bit_of(device_ref, k):
    return device_ref[0] >> k & 1


def cost(flops, moved):
    return pl.CostEstimate(flops=flops, bytes_accessed=moved, transcendentals=0)


def strength_of(bond_ref, bond, scale):
    return bond_ref[bond].astype(jnp.float32) * (0.5 * COUPLING_STEP * scale)


def tile_of(ref, t):
    return ref[:, t * LANES : (t + 1) * LANES]


def across(ref, t, bit):
    if bit >= LANE_BITS:
        return tile_of(ref, t ^ (1 << bit - LANE_BITS))
    values = tile_of(ref, t)
    lane = lax.broadcasted_iota(jnp.int32, values.shape, 1)
    return jnp.where(lane >> bit & 1 == 1, pltpu.roll(values, 1 << bit, 1), pltpu.roll(values, LANES - (1 << bit), 1))


def sided(pair, t, bit):
    if bit >= LANE_BITS:
        return pair[t >> bit - LANE_BITS & 1]
    lane = lax.broadcasted_iota(jnp.int32, (1, LANES), 1)
    return jnp.where(lane >> bit & 1 == 1, pair[1], pair[0])


def local_kernel(device_ref, field_ref, bond_ref, x_ref, prev_ref, out_ref, *, global_bits, scale):
    vectors, amp_count = x_ref.shape
    local_bits = amp_count.bit_length() - 1
    rest_bits = local_bits - global_bits
    site_count = field_ref.shape[0]
    tile_bits = local_bits - LANE_BITS

    def position(site):
        if site >= local_bits:
            return site
        return rest_bits + site if site < global_bits else site - global_bits

    fields = [field_ref[s].astype(jnp.float32) * (FIELD_STEP * scale) for s in range(site_count)]
    couplings = [bond_ref[s].astype(jnp.float32) * COUPLING_STEP for s in range(site_count - 1)]
    scaled = [value * scale for value in couplings]
    lane = lax.broadcasted_iota(jnp.int32, (1, LANES), 1)
    lane_spin = [0.5 - (lane >> k & 1).astype(jnp.float32) for k in range(LANE_BITS)]
    far_spin = [0.5 - bit_of(device_ref, k).astype(jnp.float32) for k in range(site_count - local_bits)]

    lane_row = jnp.zeros((1, LANES), jnp.float32)
    rest = jnp.float32(0.0)
    fields_of = [jnp.float32(0.0)] * tile_bits
    bonds_of = [[] for _ in range(tile_bits)]
    mixed = []
    for s in range(site_count):
        spot = position(s)
        if spot < LANE_BITS:
            lane_row = lane_row + fields[s] * lane_spin[spot]
        elif spot < local_bits:
            fields_of[spot - LANE_BITS] = fields_of[spot - LANE_BITS] + fields[s]
        else:
            rest = rest + fields[s] * far_spin[spot - local_bits]
        if s == site_count - 1:
            continue
        low, high = sorted((spot, position(s + 1)))
        if high < LANE_BITS:
            lane_row = lane_row + scaled[s] * (lane_spin[low] * lane_spin[high])
        elif high < local_bits and low >= LANE_BITS:
            bonds_of[high - LANE_BITS].append((low - LANE_BITS, scaled[s]))
        elif high < local_bits:
            mixed.append((high - LANE_BITS, scaled[s] * lane_spin[low]))
        elif low >= local_bits:
            rest = rest + scaled[s] * (far_spin[low - local_bits] * far_spin[high - local_bits])
        elif low >= LANE_BITS:
            fields_of[low - LANE_BITS] = fields_of[low - LANE_BITS] + scaled[s] * far_spin[high - local_bits]
        else:
            lane_row = lane_row + scaled[s] * far_spin[high - local_bits] * lane_spin[low]
    number = [rest]
    for k in range(tile_bits):
        longer = []
        for up in (0, 1):
            for t, value in enumerate(number):
                term = (0.5 - up) * fields_of[k]
                for other, coupling in bonds_of[k]:
                    term = term + (0.5 - up) * (0.5 - (t >> other & 1)) * coupling
                longer.append(value + term)
        number = longer
    mixed_bits = sorted({bit for bit, _ in mixed})
    lane_rows = {}
    for pattern in range(1 << len(mixed_bits)):
        row = lane_row
        for bit, vector in mixed:
            row = row + (0.5 - (pattern >> mixed_bits.index(bit) & 1)) * vector
        lane_rows[pattern] = row

    rows = lax.broadcasted_iota(jnp.int32, (GROUP, GROUP), 0)
    cols = lax.broadcasted_iota(jnp.int32, (GROUP, GROUP), 1)
    change = rows ^ cols
    matrix = jnp.zeros((GROUP, GROUP), jnp.float32)
    tile_bonds, wraps = [], []
    for s in range(local_bits - 1):
        low, high = sorted((position(s), position(s + 1)))
        if high < GROUP_BITS:
            chosen = (change == (1 << low | 1 << high)) & ((cols >> low & 1) != (cols >> high & 1))
            matrix = jnp.where(chosen, 0.5 * couplings[s], matrix)
        elif low >= LANE_BITS:
            tile_bonds.append((low - LANE_BITS, high - LANE_BITS, 0.5 * scaled[s]))
        else:
            shown = [jnp.where((lane >> low & 1) != up, 0.5 * scaled[s], 0.0) for up in (0, 1)]
            wraps.append((high - LANE_BITS, low, shown))
    matrix = matrix.astype(jnp.bfloat16)
    stacked = jnp.concatenate([x_ref[:, k * GROUP : (k + 1) * GROUP] for k in range(amp_count // GROUP)], axis=0)
    product = None
    for part in pieces(stacked, 3):
        term = jnp.dot(part, matrix, preferred_element_type=jnp.float32)
        product = term if product is None else product + term

    def tile(t):
        return x_ref[:, t * LANES : (t + 1) * LANES]

    for t in range(amp_count // LANES):
        row = t // 2 * vectors
        side = (t & 1) * LANES
        pattern = sum((t >> bit & 1) << j for j, bit in enumerate(mixed_bits))
        total = (lane_rows[pattern] + number[t]) * tile(t) - prev_ref[:, t * LANES : (t + 1) * LANES]
        total = total + scale * product[row : row + vectors, side : side + LANES]
        for one, two, weight in tile_bonds:
            if (t >> one & 1) != (t >> two & 1):
                total = total + weight * tile(t ^ (1 << one) ^ (1 << two))
        for high, low, shown in wraps:
            up = t >> high & 1
            shift = 1 << low if up == 0 else LANES - (1 << low)
            total = total + shown[up] * pltpu.roll(tile(t ^ (1 << high)), shift, 1)
        out_ref[:, t * LANES : (t + 1) * LANES] = total


def cut_kernel(x_ref, out_ref, sems, *, start):
    rows, width = out_ref.shape
    copies = []
    for k in range(rows // SUBLANES):
        strip = pl.ds(k * SUBLANES, SUBLANES)
        copies.append(
            pltpu.make_async_copy(x_ref.at[strip, pl.ds(start, width)], out_ref.at[strip], sems.at[k])
        )
        copies[-1].start()
    for copy in copies:
        copy.wait()


def cut(values, start, width):
    rows = values.shape[0]
    return pl.pallas_call(
        functools.partial(cut_kernel, start=start),
        out_shape=jax.ShapeDtypeStruct((rows, width), values.dtype),
        in_specs=[pl.BlockSpec(memory_space=pltpu.HBM)],
        out_specs=pl.BlockSpec(memory_space=pltpu.VMEM),
        scratch_shapes=[pltpu.SemaphoreType.DMA((rows // SUBLANES,))],
        compiler_params=params(CUT_LIMIT),
        cost_estimate=cost(0, 8 * rows * width),
        name=f"cut_{start}",
    )(values)


def ready_kernel(device_ref, bond_ref, own_ref, swap_ref, *out_refs, bit, bond, scale):
    p, m, q = (bit_of(device_ref, k) for k in range(3))
    joint, low = (strength_of(bond_ref, bond + k, scale) for k in range(2))
    low = jnp.where((p != m) & (q != m), low, 0.0)
    passing = (p != m) & (q == m)
    corner = (p == m) & (q == m)
    swap_pair = [jnp.where(passing & (p == side), joint, 0.0) for side in (0, 1)]
    own_pair = [jnp.where(corner & (p == side), joint, 0.0) for side in (0, 1)]
    t = 0
    for out_ref in out_refs:
        for place in range(out_ref.shape[1] // LANES):
            total = low * tile_of(swap_ref, t) + sided(swap_pair, t, bit) * across(swap_ref, t, bit)
            total = total + sided(own_pair, t, bit) * across(own_ref, t, bit)
            out_ref[:, place * LANES : (place + 1) * LANES] = total
            t += 1


def later_ready_kernel(device_ref, bond_ref, swap_ref, *out_refs, middle, bond, scale):
    p, m, q = (bit_of(device_ref, middle + k) for k in (-1, 0, 1))
    low = jnp.where((p == m) & (q == m), strength_of(bond_ref, bond, scale), 0.0)
    first = 0
    for out_ref in out_refs:
        out_ref[...] = low * swap_ref[:, first : first + out_ref.shape[1]]
        first += out_ref.shape[1]


def later_sent_kernel(bond_ref, ready_ref, arrived_ref, out_ref, *, bond, scale):
    out_ref[...] = ready_ref[...] + strength_of(bond_ref, bond, scale) * arrived_ref[...]


def sent_kernel(device_ref, bond_ref, ready_ref, arrived_ref, out_ref, *, bond, scale):
    high = strength_of(bond_ref, bond + 2, scale)
    high = jnp.where(bit_of(device_ref, 0) != bit_of(device_ref, 1), high, 0.0)
    out_ref[...] = ready_ref[...] + high * arrived_ref[...]


def gather_kernel(device_ref, bond_ref, local_ref, first_ref, *refs, start, bit, local_bits, scale):
    out_ref = refs[-1]
    p, m, q = (bit_of(device_ref, k) for k in range(3))
    joint, low = (strength_of(bond_ref, local_bits - 1 + k, scale) for k in range(2))
    low = jnp.where((p != m) & (q == m), low, 0.0)
    halves = ((p == m) & (q == m)) | ((p != m) & (q != m))
    pair = [jnp.where(halves & (p != side), joint, 0.0) for side in (0, 1)]
    weights = []
    for k in range(len(refs) - 1):
        p, m, q = (bit_of(device_ref, 2 * k + j) for j in (2, 3, 4))
        weight = strength_of(bond_ref, local_bits + 2 * k + 2, scale)
        weights.append(jnp.where((p != m) & (q == m), weight, 0.0))
    for t in range(out_ref.shape[1] // LANES):
        total = tile_of(local_ref, start + t) + low * tile_of(first_ref, t)
        total = total + sided(pair, t, bit) * across(first_ref, t, bit)
        for weight, ref in zip(weights, refs):
            total = total + weight * tile_of(ref, t)
        out_ref[:, t * LANES : (t + 1) * LANES] = total


def packed(gram, vectors):
    fold = max(1, LANES // vectors)
    rows = vectors // fold
    return jnp.concatenate([gram[k * rows : (k + 1) * rows, :] for k in range(fold)], axis=1)


def unpacked(table, vectors):
    fold = max(1, LANES // vectors)
    return jnp.concatenate([table[:, k * vectors : (k + 1) * vectors] for k in range(fold)], axis=0)


def add_kernel(one_ref, two_ref, out_ref):
    out_ref[...] = one_ref[...] + two_ref[...]


def filter_kernel(before_ref, acc_ref, *refs, share, last):
    out_ref, gram_ref = refs[-2:]
    vectors, amp_count = acc_ref.shape
    table = before_ref[...]
    for first in range(0, amp_count, CHUNK):
        cols = slice(first, min(first + CHUNK, amp_count))
        total = acc_ref[:, cols]
        for ref in refs[:-2]:
            total = total + ref[:, cols]
        out_ref[:, cols] = total
        stacked = jnp.concatenate(pieces(total, 3), axis=0)
        table = table + lax.dot_general(
            stacked, stacked, (((1,), (1,)), ((), ())), preferred_element_type=jnp.float32
        )
    if not last:
        gram_ref[...] = table
        return

    def block(a, b):
        return table[a * vectors : (a + 1) * vectors, b * vectors : (b + 1) * vectors]

    gram = block(0, 0) + (block(0, 1) + block(1, 0)) + (block(1, 1) + (block(0, 2) + block(2, 0)))
    gram_ref[...] = packed(gram * share, vectors)


def reciprocal(values):
    guess = pl.reciprocal(values, approx=True)
    return guess * (2.0 - values * guess)


def factor(gram):
    vectors = gram.shape[0]
    lanes = max(LANES, 2 * vectors)
    rows = lax.broadcasted_iota(jnp.int32, (vectors, lanes), 0)
    cols = lax.broadcasted_iota(jnp.int32, (vectors, lanes), 1)
    rest = jnp.concatenate([gram, jnp.zeros((vectors, lanes - vectors), jnp.float32)], axis=1)
    rest = rest + (cols == rows + vectors).astype(jnp.float32)
    for panel in range(0, vectors, PANEL):
        columns = [jnp.broadcast_to(rest[:, k : k + 1], rest.shape) for k in range(panel, min(panel + PANEL, vectors))]
        for k in range(0, len(columns), 2):
            i, j = panel + k, panel + k + 1
            left, right = columns[k : k + 2]
            a, b, d = left[i:j, :], left[j : j + 1, :], right[j : j + 1, :]
            scale = reciprocal(a * d - b * b)
            left = jnp.where(rows > j, left, 0.0)
            right = jnp.where(rows > j, right, 0.0)

            def eliminate(values):
                one, two = values[i:j, :], values[j : j + 1, :]
                return values - (left * ((d * one - b * two) * scale) + right * ((a * two - b * one) * scale))

            columns[k + 2 :] = [eliminate(values) for values in columns[k + 2 :]]
            rest = eliminate(rest)
    diagonal = jnp.sum(jnp.where(cols == rows, rest, 0.0), axis=1, keepdims=True)
    odd = (rows & 1) == 1
    corner = jnp.sum(jnp.where((cols == rows - 1) & odd, rest, 0.0), axis=1, keepdims=True)
    before = pltpu.roll(rest, 1, 0)
    lead = pltpu.roll(jnp.broadcast_to(diagonal, rest.shape), 1, 0)
    ratio = jnp.where(odd, corner * reciprocal(lead), 0.0)
    rest = (rest - ratio * before) * lax.rsqrt(diagonal - corner * ratio)
    return jnp.where(cols >= rows, rest, 0.0)[:, :vectors], rest[:, vectors : 2 * vectors]


def finish_kernel(gram_ref, *refs):
    out_ref, upper_ref, held_ref, sems = refs[-4:]
    vectors = out_ref.shape[0]
    upper, inverse = factor(unpacked(gram_ref[...], vectors))
    upper_ref[...] = upper
    high, middle, low = pieces(inverse, 3)
    none = jnp.zeros_like(high)
    left = jnp.concatenate(
        [
            jnp.concatenate([high, high, high, low], axis=1),
            jnp.concatenate([middle, middle, none, none], axis=1),
        ],
        axis=0,
    )
    copies = []
    place = 0
    for ref in refs[:-4]:
        for first in range(0, ref.shape[1], OUT_CHUNK):
            count = min(OUT_CHUNK, ref.shape[1] - first)
            right = pieces(ref[:, first : first + count], 3)
            product = jnp.dot(left, jnp.concatenate(right + right[:1], axis=0), preferred_element_type=jnp.float32)
            held_ref[:, place : place + count] = product[:vectors] + product[vectors:]
            cols = pl.ds(place, count)
            copies.append(
                pltpu.make_async_copy(held_ref.at[:, cols], out_ref.at[:, cols], sems.at[len(copies)])
            )
            copies[-1].start()
            place += count
    for copy in copies:
        copy.wait()


def local(previous, current, field_levels, bond_levels, lo_bits):
    vectors, amp_count = current.shape
    site_count = field_levels.shape[0]
    devices = lax.axis_size("hi") * lax.axis_size("lo")
    local_bits = amp_count.bit_length() - 1
    global_bits = devices.bit_length() - 1
    rest_bits = local_bits - global_bits
    device = lax.axis_index("hi") * lax.axis_size("lo") + lax.axis_index("lo")
    place = device.astype(jnp.int32).reshape(1)
    scale = 4.0 / site_count
    whole = jax.ShapeDtypeStruct((vectors, amp_count), jnp.float32)
    size = vectors * amp_count
    vmem = pl.BlockSpec(memory_space=pltpu.VMEM)

    def permute(values, pairs):
        return lax.ppermute(values, AXES, pairs)

    def flips(mask, keep=lambda i: True):
        return [(i, i ^ mask) for i in range(devices) if keep(i)]

    def strength(bond):
        return (scale * 0.5 * COUPLING_STEP) * bond_levels[bond].astype(jnp.float32)

    middles = tuple(range(3, global_bits - 1, 2))
    width = amp_count // 32
    parts = [(0, 20), (20, 12)]
    swaps = [permute(current, flips(1 << m - 1)) for m in middles or (3,)]
    firsts, boths = [], []
    for start, count in parts:
        piece = cut(current, start * width, count * width)
        firsts.append(permute(piece, route(devices, 1, FIRST)))
        boths.append([permute(piece, route(devices, m, LATER_FIRST)) for m in middles])

    current, _ = lax.optimization_barrier((current, piece))

    here = pl.pallas_call(
        functools.partial(local_kernel, global_bits=global_bits, scale=scale),
        out_shape=whole,
        in_specs=[smem()] * 3 + [vmem] * 2,
        out_specs=vmem,
        compiler_params=params(),
        cost_estimate=cost(6 * size * GROUP, 12 * size),
        name="local_bonds",
    )(place, field_levels, bond_levels, current, previous)
    ready = pl.pallas_call(
        functools.partial(ready_kernel, bit=rest_bits - 1, bond=local_bits - 1, scale=scale),
        out_shape=tuple(jax.ShapeDtypeStruct((vectors, count * width), jnp.float32) for _, count in parts),
        in_specs=[smem()] * 2 + [vmem] * 2,
        out_specs=tuple(vmem for _ in parts),
        compiler_params=params(),
        cost_estimate=cost(6 * size, 12 * size),
        name="ready",
    )(place, bond_levels, current, swaps[0])
    later_ready = [
        pl.pallas_call(
            functools.partial(later_ready_kernel, middle=m, bond=local_bits + m - 1, scale=scale),
            out_shape=tuple(jax.ShapeDtypeStruct((vectors, count * width), jnp.float32) for _, count in parts),
            in_specs=[smem()] * 2 + [vmem],
            out_specs=tuple(vmem for _ in parts),
            compiler_params=params(),
            cost_estimate=cost(size, 8 * size),
            name=f"ready_{m}",
        )(place, bond_levels, swap)
        for m, swap in zip(middles, swaps)
    ]
    firsts[0], here, ready, later_ready = lax.optimization_barrier((firsts[0], here, ready, later_ready))
    if global_bits % 2 == 0:
        top = global_bits - 1
        moved = permute(current, flips(3 << top - 1, lambda i: (i >> top & 1) != (i >> top - 1 & 1)))
        here = here + strength(site_count - 2) * moved

    seconds, ons, accs, sents = [], [], [], []
    for number, ((start, count), first, both, base) in enumerate(zip(parts, firsts, boths, ready)):
        shape = jax.ShapeDtypeStruct((vectors, count * width), jnp.float32)
        part_size = vectors * count * width
        sent = pl.pallas_call(
            functools.partial(sent_kernel, bond=local_bits - 1, scale=scale),
            out_shape=shape,
            in_specs=[smem()] * 2 + [vmem] * 2,
            out_specs=vmem,
            compiler_params=params(),
            cost_estimate=cost(0, 0),
            name=f"sent_on_{start}",
        )(place, bond_levels, base, first)
        seconds.append(permute(sent, route(devices, 1, SECOND)))
        sents.append(sent)
        arrived, sent = lax.optimization_barrier((both, sent))
        on = []
        for m, values, bases in zip(middles, arrived, later_ready):
            sent = pl.pallas_call(
                functools.partial(later_sent_kernel, bond=local_bits + m, scale=scale),
                out_shape=shape,
                in_specs=[smem()] + [vmem] * 2,
                out_specs=vmem,
                compiler_params=params(),
                cost_estimate=cost(0, 0),
                name=f"sent_{m}_{start}",
            )(bond_levels, bases[number], values)
            on.append(permute(sent, route(devices, m, LATER_SECOND)))
        ons.append(on)
    firsts, sents = lax.optimization_barrier((firsts, sents))
    for (start, count), first, both in zip(parts, firsts, boths):
        shape = jax.ShapeDtypeStruct((vectors, count * width), jnp.float32)
        part_size = vectors * count * width
        accs.append(
            pl.pallas_call(
                functools.partial(
                    gather_kernel, start=start * width // LANES, bit=rest_bits - 1, local_bits=local_bits, scale=scale
                ),
                out_shape=shape,
                in_specs=[smem()] * 2 + [vmem] * (2 + len(both)),
                out_specs=vmem,
                compiler_params=params(),
                cost_estimate=cost(0, 0),
                name=f"gather_first_{start}",
            )(place, bond_levels, here, first, *both)
        )

    fold = max(1, LANES // vectors)
    table = (vectors // fold, vectors * fold)
    square = (3 * vectors, 3 * vectors)
    filtered = []
    products = jnp.zeros(square, jnp.float32)
    for number, ((start, count), acc, second, on) in enumerate(zip(parts, accs, seconds, ons)):
        last = number == len(parts) - 1
        part_size = vectors * count * width
        second, products = lax.optimization_barrier((second, products))
        acc = pl.pallas_call(
            add_kernel,
            out_shape=jax.ShapeDtypeStruct((vectors, count * width), jnp.float32),
            in_specs=[vmem] * 2,
            out_specs=vmem,
            compiler_params=params(),
            cost_estimate=cost(ADD_COST, 0),
            name=f"add_{start}",
        )(acc, second)
        done, products = pl.pallas_call(
            functools.partial(filter_kernel, share=1.0 / (amp_count * devices), last=last),
            out_shape=(
                jax.ShapeDtypeStruct((vectors, count * width), jnp.float32),
                jax.ShapeDtypeStruct(table if last else square, jnp.float32),
            ),
            in_specs=[vmem] * (2 + len(on)),
            out_specs=(vmem, vmem),
            compiler_params=params(),
            cost_estimate=cost(6 * part_size * vectors, 16 * part_size),
            name=f"filter_gram_{start}",
        )(products, acc, *on)
        filtered.append(done)
    gram = products

    hub = 1 << lo_bits
    gram = gram + permute(gram, flips(hub))
    for k in [k for k in range(global_bits) if k > lo_bits] + list(range(lo_bits)):
        gram = gram + permute(gram, flips(1 << k | hub))

    chunks = sum(-(-values.shape[1] // OUT_CHUNK) for values in filtered)
    return pl.pallas_call(
        finish_kernel,
        out_shape=(whole, jax.ShapeDtypeStruct((vectors, vectors), jnp.float32)),
        in_specs=[vmem] * (1 + len(filtered)),
        out_specs=(pl.BlockSpec(memory_space=pltpu.HBM), vmem),
        scratch_shapes=[pltpu.VMEM((vectors, amp_count), jnp.float32), pltpu.SemaphoreType.DMA((chunks,))],
        compiler_params=params(),
        cost_estimate=cost(12 * size * vectors, 8 * size),
        name="factor_apply",
    )(gram, *filtered)


def solution(mesh):
    in_specs = (P(None, AXES), P(None, AXES), P(), P())
    out_specs = (P(None, AXES), P())
    lo_bits = mesh.shape["lo"].bit_length() - 1
    return jax.shard_map(
        functools.partial(local, lo_bits=lo_bits), mesh=mesh, in_specs=in_specs, out_specs=out_specs, check_vma=False
    )
```

```python
import functools

import jax
import jax.numpy as jnp
from jax import lax
from jax.experimental import pallas as pl
from jax.experimental.pallas import tpu as pltpu
from jax.sharding import PartitionSpec as P

FIELD_STEP = 0.75
COUPLING_STEP = 0.5
AXES = ("hi", "lo")
LANES = 128
SUBLANES = 8
LANE_BITS = 7
GROUP = 256
CHUNK = 1024
OUT_CHUNK = 2048
PANEL = 16
GROUP_BITS = 8
VMEM_LIMIT = 28 * 1024 * 1024
ADD_COST = 10**9
CUT_LIMIT = 56 * 1024 * 1024


def pieces(values, count):
    parts = []
    for _ in range(count):
        part = values.astype(jnp.bfloat16)
        parts.append(part)
        values = values - part.astype(jnp.float32)
    return parts


def smem():
    return pl.BlockSpec(memory_space=pltpu.SMEM)


def params(limit=VMEM_LIMIT):
    return pltpu.CompilerParams(vmem_limit_bytes=limit)


FIRST = {(0, 1, 0): (1, 0, 0), (1, 1, 0): (0, 1, 0), (1, 0, 0): (0, 0, 0), (0, 0, 0): (0, 0, 1)}
SECOND = {(0, 1, 0): (1, 0, 1), (1, 0, 0): (0, 0, 1), (0, 0, 0): (1, 0, 0), (1, 1, 0): (1, 1, 1)}
LATER_FIRST = {(0, 1, 0): (1, 0, 0), (1, 1, 0): (1, 1, 1)}
LATER_SECOND = {(1, 1, 1): (1, 0, 1), (1, 0, 0): (0, 0, 1)}


def route(devices, m, table):
    full = {}
    for one, two in table.items():
        full[one] = two
        full[tuple(1 - b for b in one)] = tuple(1 - b for b in two)
    pairs = []
    for device in range(devices):
        goal = full.get(tuple(device >> m + j & 1 for j in (-1, 0, 1)))
        if goal is None:
            continue
        pairs.append((device, device & ~(7 << m - 1) | goal[0] << m - 1 | goal[1] << m | goal[2] << m + 1))
    return pairs


def bit_of(device_ref, k):
    return device_ref[0] >> k & 1


def cost(flops, moved):
    return pl.CostEstimate(flops=flops, bytes_accessed=moved, transcendentals=0)


def strength_of(bond_ref, bond, scale):
    return bond_ref[bond].astype(jnp.float32) * (0.5 * COUPLING_STEP * scale)


def tile_of(ref, t):
    return ref[:, t * LANES : (t + 1) * LANES]


def across(ref, t, bit):
    if bit >= LANE_BITS:
        return tile_of(ref, t ^ (1 << bit - LANE_BITS))
    values = tile_of(ref, t)
    lane = lax.broadcasted_iota(jnp.int32, values.shape, 1)
    return jnp.where(lane >> bit & 1 == 1, pltpu.roll(values, 1 << bit, 1), pltpu.roll(values, LANES - (1 << bit), 1))


def sided(pair, t, bit):
    if bit >= LANE_BITS:
        return pair[t >> bit - LANE_BITS & 1]
    lane = lax.broadcasted_iota(jnp.int32, (1, LANES), 1)
    return jnp.where(lane >> bit & 1 == 1, pair[1], pair[0])


def local_kernel(device_ref, field_ref, bond_ref, x_ref, prev_ref, out_ref, *, global_bits, scale):
    vectors, amp_count = x_ref.shape
    local_bits = amp_count.bit_length() - 1
    rest_bits = local_bits - global_bits
    site_count = field_ref.shape[0]
    tile_bits = local_bits - LANE_BITS

    def position(site):
        if site >= local_bits:
            return site
        return rest_bits + site if site < global_bits else site - global_bits

    fields = [field_ref[s].astype(jnp.float32) * (FIELD_STEP * scale) for s in range(site_count)]
    couplings = [bond_ref[s].astype(jnp.float32) * COUPLING_STEP for s in range(site_count - 1)]
    scaled = [value * scale for value in couplings]
    lane = lax.broadcasted_iota(jnp.int32, (1, LANES), 1)
    lane_spin = [0.5 - (lane >> k & 1).astype(jnp.float32) for k in range(LANE_BITS)]
    far_spin = [0.5 - bit_of(device_ref, k).astype(jnp.float32) for k in range(site_count - local_bits)]

    lane_row = jnp.zeros((1, LANES), jnp.float32)
    rest = jnp.float32(0.0)
    fields_of = [jnp.float32(0.0)] * tile_bits
    bonds_of = [[] for _ in range(tile_bits)]
    mixed = []
    for s in range(site_count):
        spot = position(s)
        if spot < LANE_BITS:
            lane_row = lane_row + fields[s] * lane_spin[spot]
        elif spot < local_bits:
            fields_of[spot - LANE_BITS] = fields_of[spot - LANE_BITS] + fields[s]
        else:
            rest = rest + fields[s] * far_spin[spot - local_bits]
        if s == site_count - 1:
            continue
        low, high = sorted((spot, position(s + 1)))
        if high < LANE_BITS:
            lane_row = lane_row + scaled[s] * (lane_spin[low] * lane_spin[high])
        elif high < local_bits and low >= LANE_BITS:
            bonds_of[high - LANE_BITS].append((low - LANE_BITS, scaled[s]))
        elif high < local_bits:
            mixed.append((high - LANE_BITS, scaled[s] * lane_spin[low]))
        elif low >= local_bits:
            rest = rest + scaled[s] * (far_spin[low - local_bits] * far_spin[high - local_bits])
        elif low >= LANE_BITS:
            fields_of[low - LANE_BITS] = fields_of[low - LANE_BITS] + scaled[s] * far_spin[high - local_bits]
        else:
            lane_row = lane_row + scaled[s] * far_spin[high - local_bits] * lane_spin[low]
    number = [rest]
    for k in range(tile_bits):
        longer = []
        for up in (0, 1):
            for t, value in enumerate(number):
                term = (0.5 - up) * fields_of[k]
                for other, coupling in bonds_of[k]:
                    term = term + (0.5 - up) * (0.5 - (t >> other & 1)) * coupling
                longer.append(value + term)
        number = longer
    mixed_bits = sorted({bit for bit, _ in mixed})
    lane_rows = {}
    for pattern in range(1 << len(mixed_bits)):
        row = lane_row
        for bit, vector in mixed:
            row = row + (0.5 - (pattern >> mixed_bits.index(bit) & 1)) * vector
        lane_rows[pattern] = row

    rows = lax.broadcasted_iota(jnp.int32, (GROUP, GROUP), 0)
    cols = lax.broadcasted_iota(jnp.int32, (GROUP, GROUP), 1)
    change = rows ^ cols
    matrix = jnp.zeros((GROUP, GROUP), jnp.float32)
    tile_bonds, wraps = [], []
    for s in range(local_bits - 1):
        low, high = sorted((position(s), position(s + 1)))
        if high < GROUP_BITS:
            chosen = (change == (1 << low | 1 << high)) & ((cols >> low & 1) != (cols >> high & 1))
            matrix = jnp.where(chosen, 0.5 * couplings[s], matrix)
        elif low >= LANE_BITS:
            tile_bonds.append((low - LANE_BITS, high - LANE_BITS, 0.5 * scaled[s]))
        else:
            shown = [jnp.where((lane >> low & 1) != up, 0.5 * scaled[s], 0.0) for up in (0, 1)]
            wraps.append((high - LANE_BITS, low, shown))
    matrix = matrix.astype(jnp.bfloat16)
    stacked = jnp.concatenate([x_ref[:, k * GROUP : (k + 1) * GROUP] for k in range(amp_count // GROUP)], axis=0)
    product = None
    for part in pieces(stacked, 3):
        term = jnp.dot(part, matrix, preferred_element_type=jnp.float32)
        product = term if product is None else product + term

    def tile(t):
        return x_ref[:, t * LANES : (t + 1) * LANES]

    for t in range(amp_count // LANES):
        row = t // 2 * vectors
        side = (t & 1) * LANES
        pattern = sum((t >> bit & 1) << j for j, bit in enumerate(mixed_bits))
        total = (lane_rows[pattern] + number[t]) * tile(t) - prev_ref[:, t * LANES : (t + 1) * LANES]
        total = total + scale * product[row : row + vectors, side : side + LANES]
        for one, two, weight in tile_bonds:
            if (t >> one & 1) != (t >> two & 1):
                total = total + weight * tile(t ^ (1 << one) ^ (1 << two))
        for high, low, shown in wraps:
            up = t >> high & 1
            shift = 1 << low if up == 0 else LANES - (1 << low)
            total = total + shown[up] * pltpu.roll(tile(t ^ (1 << high)), shift, 1)
        out_ref[:, t * LANES : (t + 1) * LANES] = total


def cut_kernel(x_ref, out_ref, held_ref, in_sems, out_sems, *, start):
    rows, width = held_ref.shape
    strips = [pl.ds(k * SUBLANES, SUBLANES) for k in range(rows // SUBLANES)]
    loads = [
        pltpu.make_async_copy(x_ref.at[strip, pl.ds(start, width)], held_ref.at[strip], in_sems.at[k])
        for k, strip in enumerate(strips)
    ]
    stores = [
        pltpu.make_async_copy(held_ref.at[strip], out_ref.at[strip], out_sems.at[k]) for k, strip in enumerate(strips)
    ]
    for load in loads:
        load.start()
    for load, store in zip(loads, stores):
        load.wait()
        store.start()
    for store in stores:
        store.wait()


def cut(values, start, width):
    rows = values.shape[0]
    hbm = pl.BlockSpec(memory_space=pltpu.HBM)
    strips = rows // SUBLANES
    return pl.pallas_call(
        functools.partial(cut_kernel, start=start),
        out_shape=jax.ShapeDtypeStruct((rows, width), values.dtype),
        in_specs=[hbm],
        out_specs=hbm,
        scratch_shapes=[
            pltpu.VMEM((rows, width), values.dtype),
            pltpu.SemaphoreType.DMA((strips,)),
            pltpu.SemaphoreType.DMA((strips,)),
        ],
        compiler_params=params(CUT_LIMIT),
        cost_estimate=cost(0, 8 * rows * width),
        name=f"cut_{start}",
    )(values)


def ready_kernel(device_ref, bond_ref, own_ref, swap_ref, *out_refs, bit, bond, scale):
    p, m, q = (bit_of(device_ref, k) for k in range(3))
    joint, low = (strength_of(bond_ref, bond + k, scale) for k in range(2))
    low = jnp.where((p != m) & (q != m), low, 0.0)
    passing = (p != m) & (q == m)
    corner = (p == m) & (q == m)
    swap_pair = [jnp.where(passing & (p == side), joint, 0.0) for side in (0, 1)]
    own_pair = [jnp.where(corner & (p == side), joint, 0.0) for side in (0, 1)]
    t = 0
    for out_ref in out_refs:
        for place in range(out_ref.shape[1] // LANES):
            total = low * tile_of(swap_ref, t) + sided(swap_pair, t, bit) * across(swap_ref, t, bit)
            total = total + sided(own_pair, t, bit) * across(own_ref, t, bit)
            out_ref[:, place * LANES : (place + 1) * LANES] = total
            t += 1


def later_ready_kernel(device_ref, bond_ref, swap_ref, *out_refs, middle, bond, scale):
    p, m, q = (bit_of(device_ref, middle + k) for k in (-1, 0, 1))
    low = jnp.where((p == m) & (q == m), strength_of(bond_ref, bond, scale), 0.0)
    first = 0
    for out_ref in out_refs:
        out_ref[...] = low * swap_ref[:, first : first + out_ref.shape[1]]
        first += out_ref.shape[1]


def later_sent_kernel(bond_ref, ready_ref, arrived_ref, out_ref, *, bond, scale):
    out_ref[...] = ready_ref[...] + strength_of(bond_ref, bond, scale) * arrived_ref[...]


def sent_kernel(device_ref, bond_ref, ready_ref, arrived_ref, out_ref, *, bond, scale):
    high = strength_of(bond_ref, bond + 2, scale)
    high = jnp.where(bit_of(device_ref, 0) != bit_of(device_ref, 1), high, 0.0)
    out_ref[...] = ready_ref[...] + high * arrived_ref[...]


def gather_kernel(device_ref, bond_ref, local_ref, first_ref, *refs, start, bit, local_bits, scale):
    out_ref = refs[-1]
    p, m, q = (bit_of(device_ref, k) for k in range(3))
    joint, low = (strength_of(bond_ref, local_bits - 1 + k, scale) for k in range(2))
    low = jnp.where((p != m) & (q == m), low, 0.0)
    halves = ((p == m) & (q == m)) | ((p != m) & (q != m))
    pair = [jnp.where(halves & (p != side), joint, 0.0) for side in (0, 1)]
    weights = []
    for k in range(len(refs) - 1):
        p, m, q = (bit_of(device_ref, 2 * k + j) for j in (2, 3, 4))
        weight = strength_of(bond_ref, local_bits + 2 * k + 2, scale)
        weights.append(jnp.where((p != m) & (q == m), weight, 0.0))
    for t in range(out_ref.shape[1] // LANES):
        total = tile_of(local_ref, start + t) + low * tile_of(first_ref, t)
        total = total + sided(pair, t, bit) * across(first_ref, t, bit)
        for weight, ref in zip(weights, refs):
            total = total + weight * tile_of(ref, t)
        out_ref[:, t * LANES : (t + 1) * LANES] = total


def packed(gram, vectors):
    fold = max(1, LANES // vectors)
    rows = vectors // fold
    return jnp.concatenate([gram[k * rows : (k + 1) * rows, :] for k in range(fold)], axis=1)


def unpacked(table, vectors):
    fold = max(1, LANES // vectors)
    return jnp.concatenate([table[:, k * vectors : (k + 1) * vectors] for k in range(fold)], axis=0)


def add_kernel(one_ref, two_ref, out_ref):
    out_ref[...] = one_ref[...] + two_ref[...]


def filter_kernel(before_ref, acc_ref, *refs, share, last):
    out_ref, gram_ref = refs[-2:]
    vectors, amp_count = acc_ref.shape
    table = before_ref[...]
    for first in range(0, amp_count, CHUNK):
        cols = slice(first, min(first + CHUNK, amp_count))
        total = acc_ref[:, cols]
        for ref in refs[:-2]:
            total = total + ref[:, cols]
        out_ref[:, cols] = total
        stacked = jnp.concatenate(pieces(total, 3), axis=0)
        table = table + lax.dot_general(
            stacked, stacked, (((1,), (1,)), ((), ())), preferred_element_type=jnp.float32
        )
    if not last:
        gram_ref[...] = table
        return

    def block(a, b):
        return table[a * vectors : (a + 1) * vectors, b * vectors : (b + 1) * vectors]

    gram = block(0, 0) + (block(0, 1) + block(1, 0)) + (block(1, 1) + (block(0, 2) + block(2, 0)))
    gram_ref[...] = packed(gram * share, vectors)


def reciprocal(values):
    guess = pl.reciprocal(values, approx=True)
    return guess * (2.0 - values * guess)


def factor(gram):
    vectors = gram.shape[0]
    lanes = max(LANES, 2 * vectors)
    rows = lax.broadcasted_iota(jnp.int32, (vectors, lanes), 0)
    cols = lax.broadcasted_iota(jnp.int32, (vectors, lanes), 1)
    rest = jnp.concatenate([gram, jnp.zeros((vectors, lanes - vectors), jnp.float32)], axis=1)
    rest = rest + (cols == rows + vectors).astype(jnp.float32)
    for panel in range(0, vectors, PANEL):
        columns = [jnp.broadcast_to(rest[:, k : k + 1], rest.shape) for k in range(panel, min(panel + PANEL, vectors))]
        for k in range(0, len(columns), 2):
            i, j = panel + k, panel + k + 1
            left, right = columns[k : k + 2]
            a, b, d = left[i:j, :], left[j : j + 1, :], right[j : j + 1, :]
            scale = reciprocal(a * d - b * b)
            left = jnp.where(rows > j, left, 0.0)
            right = jnp.where(rows > j, right, 0.0)

            def eliminate(values):
                one, two = values[i:j, :], values[j : j + 1, :]
                return values - (left * ((d * one - b * two) * scale) + right * ((a * two - b * one) * scale))

            columns[k + 2 :] = [eliminate(values) for values in columns[k + 2 :]]
            rest = eliminate(rest)
    diagonal = jnp.sum(jnp.where(cols == rows, rest, 0.0), axis=1, keepdims=True)
    odd = (rows & 1) == 1
    corner = jnp.sum(jnp.where((cols == rows - 1) & odd, rest, 0.0), axis=1, keepdims=True)
    before = pltpu.roll(rest, 1, 0)
    lead = pltpu.roll(jnp.broadcast_to(diagonal, rest.shape), 1, 0)
    ratio = jnp.where(odd, corner * reciprocal(lead), 0.0)
    rest = (rest - ratio * before) * lax.rsqrt(diagonal - corner * ratio)
    return jnp.where(cols >= rows, rest, 0.0)[:, :vectors], rest[:, vectors : 2 * vectors]


def finish_kernel(gram_ref, *refs):
    out_ref, upper_ref, held_ref, sems = refs[-4:]
    vectors = out_ref.shape[0]
    upper, inverse = factor(unpacked(gram_ref[...], vectors))
    upper_ref[...] = upper
    high, middle, low = pieces(inverse, 3)
    none = jnp.zeros_like(high)
    left = jnp.concatenate(
        [
            jnp.concatenate([high, high, high, low], axis=1),
            jnp.concatenate([middle, middle, none, none], axis=1),
        ],
        axis=0,
    )
    copies = []
    place = 0
    for ref in refs[:-4]:
        for first in range(0, ref.shape[1], OUT_CHUNK):
            count = min(OUT_CHUNK, ref.shape[1] - first)
            right = pieces(ref[:, first : first + count], 3)
            product = jnp.dot(left, jnp.concatenate(right + right[:1], axis=0), preferred_element_type=jnp.float32)
            held_ref[:, place : place + count] = product[:vectors] + product[vectors:]
            cols = pl.ds(place, count)
            copies.append(
                pltpu.make_async_copy(held_ref.at[:, cols], out_ref.at[:, cols], sems.at[len(copies)])
            )
            copies[-1].start()
            place += count
    for copy in copies:
        copy.wait()


def local(previous, current, field_levels, bond_levels, lo_bits):
    vectors, amp_count = current.shape
    site_count = field_levels.shape[0]
    devices = lax.axis_size("hi") * lax.axis_size("lo")
    local_bits = amp_count.bit_length() - 1
    global_bits = devices.bit_length() - 1
    rest_bits = local_bits - global_bits
    device = lax.axis_index("hi") * lax.axis_size("lo") + lax.axis_index("lo")
    place = device.astype(jnp.int32).reshape(1)
    scale = 4.0 / site_count
    whole = jax.ShapeDtypeStruct((vectors, amp_count), jnp.float32)
    size = vectors * amp_count
    vmem = pl.BlockSpec(memory_space=pltpu.VMEM)

    def permute(values, pairs):
        return lax.ppermute(values, AXES, pairs)

    def flips(mask, keep=lambda i: True):
        return [(i, i ^ mask) for i in range(devices) if keep(i)]

    def strength(bond):
        return (scale * 0.5 * COUPLING_STEP) * bond_levels[bond].astype(jnp.float32)

    middles = tuple(range(3, global_bits - 1, 2))
    width = amp_count // 32
    parts = [(0, 20), (20, 12)]
    swaps = [permute(current, flips(1 << m - 1)) for m in middles or (3,)]
    firsts, boths = [], []
    for start, count in parts:
        piece = cut(current, start * width, count * width)
        firsts.append(permute(piece, route(devices, 1, FIRST)))
        boths.append([permute(piece, route(devices, m, LATER_FIRST)) for m in middles])

    current, _ = lax.optimization_barrier((current, piece))

    here = pl.pallas_call(
        functools.partial(local_kernel, global_bits=global_bits, scale=scale),
        out_shape=whole,
        in_specs=[smem()] * 3 + [vmem] * 2,
        out_specs=vmem,
        compiler_params=params(),
        cost_estimate=cost(6 * size * GROUP, 12 * size),
        name="local_bonds",
    )(place, field_levels, bond_levels, current, previous)
    ready = pl.pallas_call(
        functools.partial(ready_kernel, bit=rest_bits - 1, bond=local_bits - 1, scale=scale),
        out_shape=tuple(jax.ShapeDtypeStruct((vectors, count * width), jnp.float32) for _, count in parts),
        in_specs=[smem()] * 2 + [vmem] * 2,
        out_specs=tuple(vmem for _ in parts),
        compiler_params=params(),
        cost_estimate=cost(6 * size, 12 * size),
        name="ready",
    )(place, bond_levels, current, swaps[0])
    later_ready = [
        pl.pallas_call(
            functools.partial(later_ready_kernel, middle=m, bond=local_bits + m - 1, scale=scale),
            out_shape=tuple(jax.ShapeDtypeStruct((vectors, count * width), jnp.float32) for _, count in parts),
            in_specs=[smem()] * 2 + [vmem],
            out_specs=tuple(vmem for _ in parts),
            compiler_params=params(),
            cost_estimate=cost(size, 8 * size),
            name=f"ready_{m}",
        )(place, bond_levels, swap)
        for m, swap in zip(middles, swaps)
    ]
    firsts[0], here, ready, later_ready = lax.optimization_barrier((firsts[0], here, ready, later_ready))
    if global_bits % 2 == 0:
        top = global_bits - 1
        moved = permute(current, flips(3 << top - 1, lambda i: (i >> top & 1) != (i >> top - 1 & 1)))
        here = here + strength(site_count - 2) * moved

    seconds, ons, accs, sents = [], [], [], []
    for number, ((start, count), first, both, base) in enumerate(zip(parts, firsts, boths, ready)):
        shape = jax.ShapeDtypeStruct((vectors, count * width), jnp.float32)
        part_size = vectors * count * width
        sent = pl.pallas_call(
            functools.partial(sent_kernel, bond=local_bits - 1, scale=scale),
            out_shape=shape,
            in_specs=[smem()] * 2 + [vmem] * 2,
            out_specs=vmem,
            compiler_params=params(),
            cost_estimate=cost(0, 0),
            name=f"sent_on_{start}",
        )(place, bond_levels, base, first)
        seconds.append(permute(sent, route(devices, 1, SECOND)))
        sents.append(sent)
        arrived, sent = lax.optimization_barrier((both, sent))
        on = []
        for m, values, bases in zip(middles, arrived, later_ready):
            sent = pl.pallas_call(
                functools.partial(later_sent_kernel, bond=local_bits + m, scale=scale),
                out_shape=shape,
                in_specs=[smem()] + [vmem] * 2,
                out_specs=vmem,
                compiler_params=params(),
                cost_estimate=cost(0, 0),
                name=f"sent_{m}_{start}",
            )(bond_levels, bases[number], values)
            on.append(permute(sent, route(devices, m, LATER_SECOND)))
        ons.append(on)
    firsts, sents = lax.optimization_barrier((firsts, sents))
    for (start, count), first, both in zip(parts, firsts, boths):
        shape = jax.ShapeDtypeStruct((vectors, count * width), jnp.float32)
        part_size = vectors * count * width
        accs.append(
            pl.pallas_call(
                functools.partial(
                    gather_kernel, start=start * width // LANES, bit=rest_bits - 1, local_bits=local_bits, scale=scale
                ),
                out_shape=shape,
                in_specs=[smem()] * 2 + [vmem] * (2 + len(both)),
                out_specs=vmem,
                compiler_params=params(),
                cost_estimate=cost(0, 0),
                name=f"gather_first_{start}",
            )(place, bond_levels, here, first, *both)
        )

    fold = max(1, LANES // vectors)
    table = (vectors // fold, vectors * fold)
    square = (3 * vectors, 3 * vectors)
    filtered = []
    products = jnp.zeros(square, jnp.float32)
    for number, ((start, count), acc, second, on) in enumerate(zip(parts, accs, seconds, ons)):
        last = number == len(parts) - 1
        part_size = vectors * count * width
        second, products = lax.optimization_barrier((second, products))
        acc = pl.pallas_call(
            add_kernel,
            out_shape=jax.ShapeDtypeStruct((vectors, count * width), jnp.float32),
            in_specs=[vmem] * 2,
            out_specs=vmem,
            compiler_params=params(),
            cost_estimate=cost(ADD_COST, 0),
            name=f"add_{start}",
        )(acc, second)
        done, products = pl.pallas_call(
            functools.partial(filter_kernel, share=1.0 / (amp_count * devices), last=last),
            out_shape=(
                jax.ShapeDtypeStruct((vectors, count * width), jnp.float32),
                jax.ShapeDtypeStruct(table if last else square, jnp.float32),
            ),
            in_specs=[vmem] * (2 + len(on)),
            out_specs=(vmem, vmem),
            compiler_params=params(),
            cost_estimate=cost(6 * part_size * vectors, 16 * part_size),
            name=f"filter_gram_{start}",
        )(products, acc, *on)
        filtered.append(done)
    gram = products

    hub = 1 << lo_bits
    upper = [1 << k for k in range(lo_bits + 1, global_bits)]
    steps = [[hub]]
    if len(upper) > 1:
        steps.append([upper[0] | hub, upper[1] | hub, upper[0] | upper[1] | hub])
        upper = upper[2:]
    steps += [[mask | hub] for mask in upper + [1 << k for k in range(lo_bits)]]
    for masks in steps:
        gram = gram + sum(permute(gram, flips(mask)) for mask in masks)

    chunks = sum(-(-values.shape[1] // OUT_CHUNK) for values in filtered)
    return pl.pallas_call(
        finish_kernel,
        out_shape=(whole, jax.ShapeDtypeStruct((vectors, vectors), jnp.float32)),
        in_specs=[vmem] * (1 + len(filtered)),
        out_specs=(pl.BlockSpec(memory_space=pltpu.HBM), vmem),
        scratch_shapes=[pltpu.VMEM((vectors, amp_count), jnp.float32), pltpu.SemaphoreType.DMA((chunks,))],
        compiler_params=params(),
        cost_estimate=cost(12 * size * vectors, 8 * size),
        name="factor_apply",
    )(gram, *filtered)


def solution(mesh):
    in_specs = (P(None, AXES), P(None, AXES), P(), P())
    out_specs = (P(None, AXES), P())
    lo_bits = mesh.shape["lo"].bit_length() - 1
    return jax.shard_map(
        functools.partial(local, lo_bits=lo_bits), mesh=mesh, in_specs=in_specs, out_specs=out_specs, check_vma=False
    )
```

```python
import functools

import jax
import jax.numpy as jnp
from jax import lax
from jax.experimental import pallas as pl
from jax.experimental.pallas import tpu as pltpu
from jax.sharding import PartitionSpec as P

FIELD_STEP = 0.75
COUPLING_STEP = 0.5
AXES = ("hi", "lo")
LANES = 128
SUBLANES = 8
LANE_BITS = 7
GROUP = 256
CHUNK = 1024
OUT_CHUNK = 2048
PANEL = 16
GROUP_BITS = 8
VMEM_LIMIT = 28 * 1024 * 1024
ADD_COST = 10**9
CUT_LIMIT = 56 * 1024 * 1024


def pieces(values, count):
    parts = []
    for _ in range(count):
        part = values.astype(jnp.bfloat16)
        parts.append(part)
        values = values - part.astype(jnp.float32)
    return parts


def smem():
    return pl.BlockSpec(memory_space=pltpu.SMEM)


def params(limit=VMEM_LIMIT):
    return pltpu.CompilerParams(vmem_limit_bytes=limit)


FIRST = {(0, 1, 0): (1, 0, 0), (1, 1, 0): (0, 1, 0), (1, 0, 0): (0, 0, 0), (0, 0, 0): (0, 0, 1)}
SECOND = {(0, 1, 0): (1, 0, 1), (1, 0, 0): (0, 0, 1), (0, 0, 0): (1, 0, 0), (1, 1, 0): (1, 1, 1)}
LATER_FIRST = {(0, 1, 0): (1, 0, 0), (1, 1, 0): (1, 1, 1)}
LATER_SECOND = {(1, 1, 1): (1, 0, 1), (1, 0, 0): (0, 0, 1)}


def route(devices, m, table):
    full = {}
    for one, two in table.items():
        full[one] = two
        full[tuple(1 - b for b in one)] = tuple(1 - b for b in two)
    pairs = []
    for device in range(devices):
        goal = full.get(tuple(device >> m + j & 1 for j in (-1, 0, 1)))
        if goal is None:
            continue
        pairs.append((device, device & ~(7 << m - 1) | goal[0] << m - 1 | goal[1] << m | goal[2] << m + 1))
    return pairs


def bit_of(device_ref, k):
    return device_ref[0] >> k & 1


def cost(flops, moved):
    return pl.CostEstimate(flops=flops, bytes_accessed=moved, transcendentals=0)


def strength_of(bond_ref, bond, scale):
    return bond_ref[bond].astype(jnp.float32) * (0.5 * COUPLING_STEP * scale)


def tile_of(ref, t):
    return ref[:, t * LANES : (t + 1) * LANES]


def across(ref, t, bit):
    if bit >= LANE_BITS:
        return tile_of(ref, t ^ (1 << bit - LANE_BITS))
    values = tile_of(ref, t)
    lane = lax.broadcasted_iota(jnp.int32, values.shape, 1)
    return jnp.where(lane >> bit & 1 == 1, pltpu.roll(values, 1 << bit, 1), pltpu.roll(values, LANES - (1 << bit), 1))


def sided(pair, t, bit):
    if bit >= LANE_BITS:
        return pair[t >> bit - LANE_BITS & 1]
    lane = lax.broadcasted_iota(jnp.int32, (1, LANES), 1)
    return jnp.where(lane >> bit & 1 == 1, pair[1], pair[0])


def local_kernel(device_ref, field_ref, bond_ref, x_ref, prev_ref, out_ref, *, global_bits, scale):
    vectors, amp_count = x_ref.shape
    local_bits = amp_count.bit_length() - 1
    rest_bits = local_bits - global_bits
    site_count = field_ref.shape[0]
    tile_bits = local_bits - LANE_BITS

    def position(site):
        if site >= local_bits:
            return site
        return rest_bits + site if site < global_bits else site - global_bits

    fields = [field_ref[s].astype(jnp.float32) * (FIELD_STEP * scale) for s in range(site_count)]
    couplings = [bond_ref[s].astype(jnp.float32) * COUPLING_STEP for s in range(site_count - 1)]
    scaled = [value * scale for value in couplings]
    lane = lax.broadcasted_iota(jnp.int32, (1, LANES), 1)
    lane_spin = [0.5 - (lane >> k & 1).astype(jnp.float32) for k in range(LANE_BITS)]
    far_spin = [0.5 - bit_of(device_ref, k).astype(jnp.float32) for k in range(site_count - local_bits)]

    lane_row = jnp.zeros((1, LANES), jnp.float32)
    rest = jnp.float32(0.0)
    fields_of = [jnp.float32(0.0)] * tile_bits
    bonds_of = [[] for _ in range(tile_bits)]
    mixed = []
    for s in range(site_count):
        spot = position(s)
        if spot < LANE_BITS:
            lane_row = lane_row + fields[s] * lane_spin[spot]
        elif spot < local_bits:
            fields_of[spot - LANE_BITS] = fields_of[spot - LANE_BITS] + fields[s]
        else:
            rest = rest + fields[s] * far_spin[spot - local_bits]
        if s == site_count - 1:
            continue
        low, high = sorted((spot, position(s + 1)))
        if high < LANE_BITS:
            lane_row = lane_row + scaled[s] * (lane_spin[low] * lane_spin[high])
        elif high < local_bits and low >= LANE_BITS:
            bonds_of[high - LANE_BITS].append((low - LANE_BITS, scaled[s]))
        elif high < local_bits:
            mixed.append((high - LANE_BITS, scaled[s] * lane_spin[low]))
        elif low >= local_bits:
            rest = rest + scaled[s] * (far_spin[low - local_bits] * far_spin[high - local_bits])
        elif low >= LANE_BITS:
            fields_of[low - LANE_BITS] = fields_of[low - LANE_BITS] + scaled[s] * far_spin[high - local_bits]
        else:
            lane_row = lane_row + scaled[s] * far_spin[high - local_bits] * lane_spin[low]
    number = [rest]
    for k in range(tile_bits):
        longer = []
        for up in (0, 1):
            for t, value in enumerate(number):
                term = (0.5 - up) * fields_of[k]
                for other, coupling in bonds_of[k]:
                    term = term + (0.5 - up) * (0.5 - (t >> other & 1)) * coupling
                longer.append(value + term)
        number = longer
    mixed_bits = sorted({bit for bit, _ in mixed})
    lane_rows = {}
    for pattern in range(1 << len(mixed_bits)):
        row = lane_row
        for bit, vector in mixed:
            row = row + (0.5 - (pattern >> mixed_bits.index(bit) & 1)) * vector
        lane_rows[pattern] = row

    rows = lax.broadcasted_iota(jnp.int32, (GROUP, GROUP), 0)
    cols = lax.broadcasted_iota(jnp.int32, (GROUP, GROUP), 1)
    change = rows ^ cols
    matrix = jnp.zeros((GROUP, GROUP), jnp.float32)
    tile_bonds, wraps = [], []
    for s in range(local_bits - 1):
        low, high = sorted((position(s), position(s + 1)))
        if high < GROUP_BITS:
            chosen = (change == (1 << low | 1 << high)) & ((cols >> low & 1) != (cols >> high & 1))
            matrix = jnp.where(chosen, 0.5 * couplings[s], matrix)
        elif low >= LANE_BITS:
            tile_bonds.append((low - LANE_BITS, high - LANE_BITS, 0.5 * scaled[s]))
        else:
            shown = [jnp.where((lane >> low & 1) != up, 0.5 * scaled[s], 0.0) for up in (0, 1)]
            wraps.append((high - LANE_BITS, low, shown))
    matrix = matrix.astype(jnp.bfloat16)
    stacked = jnp.concatenate([x_ref[:, k * GROUP : (k + 1) * GROUP] for k in range(amp_count // GROUP)], axis=0)
    product = None
    for part in pieces(stacked, 3):
        term = jnp.dot(part, matrix, preferred_element_type=jnp.float32)
        product = term if product is None else product + term

    def tile(t):
        return x_ref[:, t * LANES : (t + 1) * LANES]

    for t in range(amp_count // LANES):
        row = t // 2 * vectors
        side = (t & 1) * LANES
        pattern = sum((t >> bit & 1) << j for j, bit in enumerate(mixed_bits))
        total = (lane_rows[pattern] + number[t]) * tile(t) - prev_ref[:, t * LANES : (t + 1) * LANES]
        total = total + scale * product[row : row + vectors, side : side + LANES]
        for one, two, weight in tile_bonds:
            if (t >> one & 1) != (t >> two & 1):
                total = total + weight * tile(t ^ (1 << one) ^ (1 << two))
        for high, low, shown in wraps:
            up = t >> high & 1
            shift = 1 << low if up == 0 else LANES - (1 << low)
            total = total + shown[up] * pltpu.roll(tile(t ^ (1 << high)), shift, 1)
        out_ref[:, t * LANES : (t + 1) * LANES] = total


def cut_kernel(x_ref, out_ref, held_ref, in_sems, out_sems, *, start):
    rows, width = held_ref.shape
    strips = [pl.ds(k * SUBLANES, SUBLANES) for k in range(rows // SUBLANES)]
    loads = [
        pltpu.make_async_copy(x_ref.at[strip, pl.ds(start, width)], held_ref.at[strip], in_sems.at[k])
        for k, strip in enumerate(strips)
    ]
    stores = [
        pltpu.make_async_copy(held_ref.at[strip], out_ref.at[strip], out_sems.at[k]) for k, strip in enumerate(strips)
    ]
    for load in loads:
        load.start()
    for load, store in zip(loads, stores):
        load.wait()
        store.start()
    for store in stores:
        store.wait()


def cut(values, start, width):
    rows = values.shape[0]
    hbm = pl.BlockSpec(memory_space=pltpu.HBM)
    strips = rows // SUBLANES
    return pl.pallas_call(
        functools.partial(cut_kernel, start=start),
        out_shape=jax.ShapeDtypeStruct((rows, width), values.dtype),
        in_specs=[hbm],
        out_specs=hbm,
        scratch_shapes=[
            pltpu.VMEM((rows, width), values.dtype),
            pltpu.SemaphoreType.DMA((strips,)),
            pltpu.SemaphoreType.DMA((strips,)),
        ],
        compiler_params=params(CUT_LIMIT),
        cost_estimate=cost(0, 8 * rows * width),
        name=f"cut_{start}",
    )(values)


def ready_kernel(device_ref, bond_ref, own_ref, swap_ref, *out_refs, bit, bond, scale):
    p, m, q = (bit_of(device_ref, k) for k in range(3))
    joint, low = (strength_of(bond_ref, bond + k, scale) for k in range(2))
    low = jnp.where((p != m) & (q != m), low, 0.0)
    passing = (p != m) & (q == m)
    corner = (p == m) & (q == m)
    swap_pair = [jnp.where(passing & (p == side), joint, 0.0) for side in (0, 1)]
    own_pair = [jnp.where(corner & (p == side), joint, 0.0) for side in (0, 1)]
    t = 0
    for out_ref in out_refs:
        for place in range(out_ref.shape[1] // LANES):
            total = low * tile_of(swap_ref, t) + sided(swap_pair, t, bit) * across(swap_ref, t, bit)
            total = total + sided(own_pair, t, bit) * across(own_ref, t, bit)
            out_ref[:, place * LANES : (place + 1) * LANES] = total
            t += 1


def later_ready_kernel(device_ref, bond_ref, swap_ref, *out_refs, middle, bond, scale):
    p, m, q = (bit_of(device_ref, middle + k) for k in (-1, 0, 1))
    low = jnp.where((p == m) & (q == m), strength_of(bond_ref, bond, scale), 0.0)
    first = 0
    for out_ref in out_refs:
        out_ref[...] = low * swap_ref[:, first : first + out_ref.shape[1]]
        first += out_ref.shape[1]


def later_sent_kernel(bond_ref, ready_ref, arrived_ref, out_ref, *, bond, scale):
    out_ref[...] = ready_ref[...] + strength_of(bond_ref, bond, scale) * arrived_ref[...]


def sent_kernel(device_ref, bond_ref, ready_ref, arrived_ref, out_ref, *, bond, scale):
    high = strength_of(bond_ref, bond + 2, scale)
    high = jnp.where(bit_of(device_ref, 0) != bit_of(device_ref, 1), high, 0.0)
    out_ref[...] = ready_ref[...] + high * arrived_ref[...]


def gather_kernel(device_ref, bond_ref, local_ref, first_ref, *refs, start, bit, local_bits, scale):
    out_ref = refs[-1]
    p, m, q = (bit_of(device_ref, k) for k in range(3))
    joint, low = (strength_of(bond_ref, local_bits - 1 + k, scale) for k in range(2))
    low = jnp.where((p != m) & (q == m), low, 0.0)
    halves = ((p == m) & (q == m)) | ((p != m) & (q != m))
    pair = [jnp.where(halves & (p != side), joint, 0.0) for side in (0, 1)]
    weights = []
    for k in range(len(refs) - 1):
        p, m, q = (bit_of(device_ref, 2 * k + j) for j in (2, 3, 4))
        weight = strength_of(bond_ref, local_bits + 2 * k + 2, scale)
        weights.append(jnp.where((p != m) & (q == m), weight, 0.0))
    for t in range(out_ref.shape[1] // LANES):
        total = tile_of(local_ref, start + t) + low * tile_of(first_ref, t)
        total = total + sided(pair, t, bit) * across(first_ref, t, bit)
        for weight, ref in zip(weights, refs):
            total = total + weight * tile_of(ref, t)
        out_ref[:, t * LANES : (t + 1) * LANES] = total


def packed(gram, vectors):
    fold = max(1, LANES // vectors)
    rows = vectors // fold
    return jnp.concatenate([gram[k * rows : (k + 1) * rows, :] for k in range(fold)], axis=1)


def unpacked(table, vectors):
    fold = max(1, LANES // vectors)
    return jnp.concatenate([table[:, k * vectors : (k + 1) * vectors] for k in range(fold)], axis=0)


def add_kernel(one_ref, two_ref, out_ref):
    out_ref[...] = one_ref[...] + two_ref[...]


def filter_kernel(before_ref, acc_ref, *refs, share, last):
    out_ref, gram_ref = refs[-2:]
    vectors, amp_count = acc_ref.shape
    table = before_ref[...]
    for first in range(0, amp_count, CHUNK):
        cols = slice(first, min(first + CHUNK, amp_count))
        total = acc_ref[:, cols]
        for ref in refs[:-2]:
            total = total + ref[:, cols]
        out_ref[:, cols] = total
        stacked = jnp.concatenate(pieces(total, 3), axis=0)
        table = table + lax.dot_general(
            stacked, stacked, (((1,), (1,)), ((), ())), preferred_element_type=jnp.float32
        )
    if not last:
        gram_ref[...] = table
        return

    def block(a, b):
        return table[a * vectors : (a + 1) * vectors, b * vectors : (b + 1) * vectors]

    gram = block(0, 0) + (block(0, 1) + block(1, 0)) + (block(1, 1) + (block(0, 2) + block(2, 0)))
    gram_ref[...] = packed(gram * share, vectors)


def reciprocal(values):
    guess = pl.reciprocal(values, approx=True)
    return guess * (2.0 - values * guess)


def factor(gram):
    vectors = gram.shape[0]
    lanes = max(LANES, 2 * vectors)
    rows = lax.broadcasted_iota(jnp.int32, (vectors, lanes), 0)
    cols = lax.broadcasted_iota(jnp.int32, (vectors, lanes), 1)
    rest = jnp.concatenate([gram, jnp.zeros((vectors, lanes - vectors), jnp.float32)], axis=1)
    rest = rest + (cols == rows + vectors).astype(jnp.float32)
    for panel in range(0, vectors, PANEL):
        columns = [jnp.broadcast_to(rest[:, k : k + 1], rest.shape) for k in range(panel, min(panel + PANEL, vectors))]
        for k in range(0, len(columns), 2):
            i, j = panel + k, panel + k + 1
            left, right = columns[k : k + 2]
            a, b, d = left[i:j, :], left[j : j + 1, :], right[j : j + 1, :]
            scale = reciprocal(a * d - b * b)
            left = jnp.where(rows > j, left, 0.0)
            right = jnp.where(rows > j, right, 0.0)

            def eliminate(values):
                one, two = values[i:j, :], values[j : j + 1, :]
                return values - (left * ((d * one - b * two) * scale) + right * ((a * two - b * one) * scale))

            columns[k + 2 :] = [eliminate(values) for values in columns[k + 2 :]]
            rest = eliminate(rest)
    diagonal = jnp.sum(jnp.where(cols == rows, rest, 0.0), axis=1, keepdims=True)
    odd = (rows & 1) == 1
    corner = jnp.sum(jnp.where((cols == rows - 1) & odd, rest, 0.0), axis=1, keepdims=True)
    before = pltpu.roll(rest, 1, 0)
    lead = pltpu.roll(jnp.broadcast_to(diagonal, rest.shape), 1, 0)
    ratio = jnp.where(odd, corner * reciprocal(lead), 0.0)
    rest = (rest - ratio * before) * lax.rsqrt(diagonal - corner * ratio)
    return jnp.where(cols >= rows, rest, 0.0)[:, :vectors], rest[:, vectors : 2 * vectors]


def finish_kernel(gram_ref, *refs):
    out_ref, upper_ref, held_ref, sems = refs[-4:]
    vectors = out_ref.shape[0]
    upper, inverse = factor(unpacked(gram_ref[...], vectors))
    upper_ref[...] = upper
    high, middle, low = pieces(inverse, 3)
    none = jnp.zeros_like(high)
    left = jnp.concatenate(
        [
            jnp.concatenate([high, high, high, low], axis=1),
            jnp.concatenate([middle, middle, none, none], axis=1),
        ],
        axis=0,
    )
    copies = []
    place = 0
    for ref in refs[:-4]:
        for first in range(0, ref.shape[1], OUT_CHUNK):
            count = min(OUT_CHUNK, ref.shape[1] - first)
            right = pieces(ref[:, first : first + count], 3)
            product = jnp.dot(left, jnp.concatenate(right + right[:1], axis=0), preferred_element_type=jnp.float32)
            held_ref[:, place : place + count] = product[:vectors] + product[vectors:]
            cols = pl.ds(place, count)
            copies.append(
                pltpu.make_async_copy(held_ref.at[:, cols], out_ref.at[:, cols], sems.at[len(copies)])
            )
            copies[-1].start()
            place += count
    for copy in copies:
        copy.wait()


def local(previous, current, field_levels, bond_levels, lo_bits):
    vectors, amp_count = current.shape
    site_count = field_levels.shape[0]
    devices = lax.axis_size("hi") * lax.axis_size("lo")
    local_bits = amp_count.bit_length() - 1
    global_bits = devices.bit_length() - 1
    rest_bits = local_bits - global_bits
    device = lax.axis_index("hi") * lax.axis_size("lo") + lax.axis_index("lo")
    place = device.astype(jnp.int32).reshape(1)
    scale = 4.0 / site_count
    whole = jax.ShapeDtypeStruct((vectors, amp_count), jnp.float32)
    size = vectors * amp_count
    vmem = pl.BlockSpec(memory_space=pltpu.VMEM)

    def permute(values, pairs):
        return lax.ppermute(values, AXES, pairs)

    def flips(mask, keep=lambda i: True):
        return [(i, i ^ mask) for i in range(devices) if keep(i)]

    def strength(bond):
        return (scale * 0.5 * COUPLING_STEP) * bond_levels[bond].astype(jnp.float32)

    middles = tuple(range(3, global_bits - 1, 2))
    width = amp_count // 32
    parts = [(0, 20), (20, 12)]
    swaps = [permute(current, flips(1 << m - 1)) for m in middles or (3,)]
    firsts, boths = [], []
    for start, count in parts:
        piece = cut(current, start * width, count * width)
        firsts.append(permute(piece, route(devices, 1, FIRST)))
        boths.append([permute(piece, route(devices, m, LATER_FIRST)) for m in middles])

    current, _ = lax.optimization_barrier((current, piece))

    here = pl.pallas_call(
        functools.partial(local_kernel, global_bits=global_bits, scale=scale),
        out_shape=whole,
        in_specs=[smem()] * 3 + [vmem] * 2,
        out_specs=vmem,
        compiler_params=params(),
        cost_estimate=cost(6 * size * GROUP, 12 * size),
        name="local_bonds",
    )(place, field_levels, bond_levels, current, previous)
    ready = pl.pallas_call(
        functools.partial(ready_kernel, bit=rest_bits - 1, bond=local_bits - 1, scale=scale),
        out_shape=tuple(jax.ShapeDtypeStruct((vectors, count * width), jnp.float32) for _, count in parts),
        in_specs=[smem()] * 2 + [vmem] * 2,
        out_specs=tuple(vmem for _ in parts),
        compiler_params=params(),
        cost_estimate=cost(6 * size, 12 * size),
        name="ready",
    )(place, bond_levels, current, swaps[0])
    later_ready = [
        pl.pallas_call(
            functools.partial(later_ready_kernel, middle=m, bond=local_bits + m - 1, scale=scale),
            out_shape=tuple(jax.ShapeDtypeStruct((vectors, count * width), jnp.float32) for _, count in parts),
            in_specs=[smem()] * 2 + [vmem],
            out_specs=tuple(vmem for _ in parts),
            compiler_params=params(),
            cost_estimate=cost(size, 8 * size),
            name=f"ready_{m}",
        )(place, bond_levels, swap)
        for m, swap in zip(middles, swaps)
    ]
    firsts[0], here, ready, later_ready = lax.optimization_barrier((firsts[0], here, ready, later_ready))
    if global_bits % 2 == 0:
        top = global_bits - 1
        moved = permute(current, flips(3 << top - 1, lambda i: (i >> top & 1) != (i >> top - 1 & 1)))
        here = here + strength(site_count - 2) * moved

    seconds, ons, accs, sents = [], [], [], []
    for number, ((start, count), first, both, base) in enumerate(zip(parts, firsts, boths, ready)):
        shape = jax.ShapeDtypeStruct((vectors, count * width), jnp.float32)
        part_size = vectors * count * width
        sent = pl.pallas_call(
            functools.partial(sent_kernel, bond=local_bits - 1, scale=scale),
            out_shape=shape,
            in_specs=[smem()] * 2 + [vmem] * 2,
            out_specs=vmem,
            compiler_params=params(),
            cost_estimate=cost(0, 0),
            name=f"sent_on_{start}",
        )(place, bond_levels, base, first)
        seconds.append(permute(sent, route(devices, 1, SECOND)))
        sents.append(sent)
        arrived, sent = lax.optimization_barrier((both, sent))
        on = []
        for m, values, bases in zip(middles, arrived, later_ready):
            sent = pl.pallas_call(
                functools.partial(later_sent_kernel, bond=local_bits + m, scale=scale),
                out_shape=shape,
                in_specs=[smem()] + [vmem] * 2,
                out_specs=vmem,
                compiler_params=params(),
                cost_estimate=cost(0, 0),
                name=f"sent_{m}_{start}",
            )(bond_levels, bases[number], values)
            on.append(permute(sent, route(devices, m, LATER_SECOND)))
        ons.append(on)
    firsts, sents = lax.optimization_barrier((firsts, sents))
    for (start, count), first, both in zip(parts, firsts, boths):
        shape = jax.ShapeDtypeStruct((vectors, count * width), jnp.float32)
        part_size = vectors * count * width
        accs.append(
            pl.pallas_call(
                functools.partial(
                    gather_kernel, start=start * width // LANES, bit=rest_bits - 1, local_bits=local_bits, scale=scale
                ),
                out_shape=shape,
                in_specs=[smem()] * 2 + [vmem] * (2 + len(both)),
                out_specs=vmem,
                compiler_params=params(),
                cost_estimate=cost(0, 0),
                name=f"gather_first_{start}",
            )(place, bond_levels, here, first, *both)
        )

    fold = max(1, LANES // vectors)
    table = (vectors // fold, vectors * fold)
    square = (3 * vectors, 3 * vectors)
    filtered = []
    products = jnp.zeros(square, jnp.float32)
    for number, ((start, count), acc, second, on) in enumerate(zip(parts, accs, seconds, ons)):
        last = number == len(parts) - 1
        part_size = vectors * count * width
        second, products = lax.optimization_barrier((second, products))
        acc = pl.pallas_call(
            add_kernel,
            out_shape=jax.ShapeDtypeStruct((vectors, count * width), jnp.float32),
            in_specs=[vmem] * 2,
            out_specs=vmem,
            compiler_params=params(),
            cost_estimate=cost(0 if last else ADD_COST, 0),
            name=f"add_{start}",
        )(acc, second)
        done, products = pl.pallas_call(
            functools.partial(filter_kernel, share=1.0 / (amp_count * devices), last=last),
            out_shape=(
                jax.ShapeDtypeStruct((vectors, count * width), jnp.float32),
                jax.ShapeDtypeStruct(table if last else square, jnp.float32),
            ),
            in_specs=[vmem] * (2 + len(on)),
            out_specs=(vmem, vmem),
            compiler_params=params(),
            cost_estimate=cost(6 * part_size * vectors, 16 * part_size),
            name=f"filter_gram_{start}",
        )(products, acc, *on)
        filtered.append(done)
    gram = products

    hub = 1 << lo_bits
    upper = [1 << k for k in range(lo_bits + 1, global_bits)]
    steps = [[hub]]
    if len(upper) > 1:
        steps.append([upper[0] | hub, upper[1] | hub, upper[0] | upper[1] | hub])
        upper = upper[2:]
    steps += [[mask | hub] for mask in upper + [1 << k for k in range(lo_bits)]]
    for masks in steps:
        gram = gram + sum(permute(gram, flips(mask)) for mask in masks)

    chunks = sum(-(-values.shape[1] // OUT_CHUNK) for values in filtered)
    return pl.pallas_call(
        finish_kernel,
        out_shape=(whole, jax.ShapeDtypeStruct((vectors, vectors), jnp.float32)),
        in_specs=[vmem] * (1 + len(filtered)),
        out_specs=(pl.BlockSpec(memory_space=pltpu.HBM), vmem),
        scratch_shapes=[pltpu.VMEM((vectors, amp_count), jnp.float32), pltpu.SemaphoreType.DMA((chunks,))],
        compiler_params=params(),
        cost_estimate=cost(12 * size * vectors, 8 * size),
        name="factor_apply",
    )(gram, *filtered)


def solution(mesh):
    in_specs = (P(None, AXES), P(None, AXES), P(), P())
    out_specs = (P(None, AXES), P())
    lo_bits = mesh.shape["lo"].bit_length() - 1
    return jax.shard_map(
        functools.partial(local, lo_bits=lo_bits), mesh=mesh, in_specs=in_specs, out_specs=out_specs, check_vma=False
    )
```

```python
import functools

import jax
import jax.numpy as jnp
from jax import lax
from jax.experimental import pallas as pl
from jax.experimental.pallas import tpu as pltpu
from jax.sharding import PartitionSpec as P

FIELD_STEP = 0.75
COUPLING_STEP = 0.5
AXES = ("hi", "lo")
LANES = 128
SUBLANES = 8
LANE_BITS = 7
GROUP = 256
CHUNK = 1024
OUT_CHUNK = 2048
PANEL = 16
GROUP_BITS = 8
VMEM_LIMIT = 28 * 1024 * 1024
ADD_COST = 10**9
CUT_LIMIT = 56 * 1024 * 1024


def pieces(values, count):
    parts = []
    for _ in range(count):
        part = values.astype(jnp.bfloat16)
        parts.append(part)
        values = values - part.astype(jnp.float32)
    return parts


def smem():
    return pl.BlockSpec(memory_space=pltpu.SMEM)


def params(limit=VMEM_LIMIT):
    return pltpu.CompilerParams(vmem_limit_bytes=limit)


FIRST = {(0, 1, 0): (1, 0, 0), (1, 1, 0): (0, 1, 0), (1, 0, 0): (0, 0, 0), (0, 0, 0): (0, 0, 1)}
SECOND = {(0, 1, 0): (1, 0, 1), (1, 0, 0): (0, 0, 1), (0, 0, 0): (1, 0, 0), (1, 1, 0): (1, 1, 1)}
LATER_FIRST = {(0, 1, 0): (1, 0, 0), (1, 1, 0): (1, 1, 1)}
LATER_SECOND = {(1, 1, 1): (1, 0, 1), (1, 0, 0): (0, 0, 1)}


def route(devices, m, table):
    full = {}
    for one, two in table.items():
        full[one] = two
        full[tuple(1 - b for b in one)] = tuple(1 - b for b in two)
    pairs = []
    for device in range(devices):
        goal = full.get(tuple(device >> m + j & 1 for j in (-1, 0, 1)))
        if goal is None:
            continue
        pairs.append((device, device & ~(7 << m - 1) | goal[0] << m - 1 | goal[1] << m | goal[2] << m + 1))
    return pairs


def bit_of(device_ref, k):
    return device_ref[0] >> k & 1


def cost(flops, moved):
    return pl.CostEstimate(flops=flops, bytes_accessed=moved, transcendentals=0)


def strength_of(bond_ref, bond, scale):
    return bond_ref[bond].astype(jnp.float32) * (0.5 * COUPLING_STEP * scale)


def tile_of(ref, t):
    return ref[:, t * LANES : (t + 1) * LANES]


def across(ref, t, bit):
    if bit >= LANE_BITS:
        return tile_of(ref, t ^ (1 << bit - LANE_BITS))
    values = tile_of(ref, t)
    lane = lax.broadcasted_iota(jnp.int32, values.shape, 1)
    return jnp.where(lane >> bit & 1 == 1, pltpu.roll(values, 1 << bit, 1), pltpu.roll(values, LANES - (1 << bit), 1))


def sided(pair, t, bit):
    if bit >= LANE_BITS:
        return pair[t >> bit - LANE_BITS & 1]
    lane = lax.broadcasted_iota(jnp.int32, (1, LANES), 1)
    return jnp.where(lane >> bit & 1 == 1, pair[1], pair[0])


def local_kernel(device_ref, field_ref, bond_ref, x_ref, prev_ref, out_ref, *, global_bits, scale):
    vectors, amp_count = x_ref.shape
    local_bits = amp_count.bit_length() - 1
    rest_bits = local_bits - global_bits
    site_count = field_ref.shape[0]
    tile_bits = local_bits - LANE_BITS

    def position(site):
        if site >= local_bits:
            return site
        return rest_bits + site if site < global_bits else site - global_bits

    fields = [field_ref[s].astype(jnp.float32) * (FIELD_STEP * scale) for s in range(site_count)]
    couplings = [bond_ref[s].astype(jnp.float32) * COUPLING_STEP for s in range(site_count - 1)]
    scaled = [value * scale for value in couplings]
    lane = lax.broadcasted_iota(jnp.int32, (1, LANES), 1)
    lane_spin = [0.5 - (lane >> k & 1).astype(jnp.float32) for k in range(LANE_BITS)]
    far_spin = [0.5 - bit_of(device_ref, k).astype(jnp.float32) for k in range(site_count - local_bits)]

    lane_row = jnp.zeros((1, LANES), jnp.float32)
    rest = jnp.float32(0.0)
    fields_of = [jnp.float32(0.0)] * tile_bits
    bonds_of = [[] for _ in range(tile_bits)]
    mixed = []
    for s in range(site_count):
        spot = position(s)
        if spot < LANE_BITS:
            lane_row = lane_row + fields[s] * lane_spin[spot]
        elif spot < local_bits:
            fields_of[spot - LANE_BITS] = fields_of[spot - LANE_BITS] + fields[s]
        else:
            rest = rest + fields[s] * far_spin[spot - local_bits]
        if s == site_count - 1:
            continue
        low, high = sorted((spot, position(s + 1)))
        if high < LANE_BITS:
            lane_row = lane_row + scaled[s] * (lane_spin[low] * lane_spin[high])
        elif high < local_bits and low >= LANE_BITS:
            bonds_of[high - LANE_BITS].append((low - LANE_BITS, scaled[s]))
        elif high < local_bits:
            mixed.append((high - LANE_BITS, scaled[s] * lane_spin[low]))
        elif low >= local_bits:
            rest = rest + scaled[s] * (far_spin[low - local_bits] * far_spin[high - local_bits])
        elif low >= LANE_BITS:
            fields_of[low - LANE_BITS] = fields_of[low - LANE_BITS] + scaled[s] * far_spin[high - local_bits]
        else:
            lane_row = lane_row + scaled[s] * far_spin[high - local_bits] * lane_spin[low]
    number = [rest]
    for k in range(tile_bits):
        longer = []
        for up in (0, 1):
            for t, value in enumerate(number):
                term = (0.5 - up) * fields_of[k]
                for other, coupling in bonds_of[k]:
                    term = term + (0.5 - up) * (0.5 - (t >> other & 1)) * coupling
                longer.append(value + term)
        number = longer
    mixed_bits = sorted({bit for bit, _ in mixed})
    lane_rows = {}
    for pattern in range(1 << len(mixed_bits)):
        row = lane_row
        for bit, vector in mixed:
            row = row + (0.5 - (pattern >> mixed_bits.index(bit) & 1)) * vector
        lane_rows[pattern] = row

    rows = lax.broadcasted_iota(jnp.int32, (GROUP, GROUP), 0)
    cols = lax.broadcasted_iota(jnp.int32, (GROUP, GROUP), 1)
    change = rows ^ cols
    matrix = jnp.zeros((GROUP, GROUP), jnp.float32)
    tile_bonds, wraps = [], []
    for s in range(local_bits - 1):
        low, high = sorted((position(s), position(s + 1)))
        if high < GROUP_BITS:
            chosen = (change == (1 << low | 1 << high)) & ((cols >> low & 1) != (cols >> high & 1))
            matrix = jnp.where(chosen, 0.5 * couplings[s], matrix)
        elif low >= LANE_BITS:
            tile_bonds.append((low - LANE_BITS, high - LANE_BITS, 0.5 * scaled[s]))
        else:
            shown = [jnp.where((lane >> low & 1) != up, 0.5 * scaled[s], 0.0) for up in (0, 1)]
            wraps.append((high - LANE_BITS, low, shown))
    matrix = matrix.astype(jnp.bfloat16)
    stacked = jnp.concatenate([x_ref[:, k * GROUP : (k + 1) * GROUP] for k in range(amp_count // GROUP)], axis=0)
    product = None
    for part in pieces(stacked, 3):
        term = jnp.dot(part, matrix, preferred_element_type=jnp.float32)
        product = term if product is None else product + term

    def tile(t):
        return x_ref[:, t * LANES : (t + 1) * LANES]

    for t in range(amp_count // LANES):
        row = t // 2 * vectors
        side = (t & 1) * LANES
        pattern = sum((t >> bit & 1) << j for j, bit in enumerate(mixed_bits))
        total = (lane_rows[pattern] + number[t]) * tile(t) - prev_ref[:, t * LANES : (t + 1) * LANES]
        total = total + scale * product[row : row + vectors, side : side + LANES]
        for one, two, weight in tile_bonds:
            if (t >> one & 1) != (t >> two & 1):
                total = total + weight * tile(t ^ (1 << one) ^ (1 << two))
        for high, low, shown in wraps:
            up = t >> high & 1
            shift = 1 << low if up == 0 else LANES - (1 << low)
            total = total + shown[up] * pltpu.roll(tile(t ^ (1 << high)), shift, 1)
        out_ref[:, t * LANES : (t + 1) * LANES] = total


def cut_kernel(x_ref, out_ref, held_ref, in_sems, out_sems, *, start):
    rows, width = held_ref.shape
    strips = [pl.ds(k * SUBLANES, SUBLANES) for k in range(rows // SUBLANES)]
    loads = [
        pltpu.make_async_copy(x_ref.at[strip, pl.ds(start, width)], held_ref.at[strip], in_sems.at[k])
        for k, strip in enumerate(strips)
    ]
    stores = [
        pltpu.make_async_copy(held_ref.at[strip], out_ref.at[strip], out_sems.at[k]) for k, strip in enumerate(strips)
    ]
    for load in loads:
        load.start()
    for load, store in zip(loads, stores):
        load.wait()
        store.start()
    for store in stores:
        store.wait()


def cut(values, start, width):
    rows = values.shape[0]
    hbm = pl.BlockSpec(memory_space=pltpu.HBM)
    strips = rows // SUBLANES
    return pl.pallas_call(
        functools.partial(cut_kernel, start=start),
        out_shape=jax.ShapeDtypeStruct((rows, width), values.dtype),
        in_specs=[hbm],
        out_specs=hbm,
        scratch_shapes=[
            pltpu.VMEM((rows, width), values.dtype),
            pltpu.SemaphoreType.DMA((strips,)),
            pltpu.SemaphoreType.DMA((strips,)),
        ],
        compiler_params=params(CUT_LIMIT),
        cost_estimate=cost(0, 8 * rows * width),
        name=f"cut_{start}",
    )(values)


def ready_kernel(device_ref, bond_ref, own_ref, swap_ref, *out_refs, bit, bond, scale):
    p, m, q = (bit_of(device_ref, k) for k in range(3))
    joint, low = (strength_of(bond_ref, bond + k, scale) for k in range(2))
    low = jnp.where((p != m) & (q != m), low, 0.0)
    passing = (p != m) & (q == m)
    corner = (p == m) & (q == m)
    swap_pair = [jnp.where(passing & (p == side), joint, 0.0) for side in (0, 1)]
    own_pair = [jnp.where(corner & (p == side), joint, 0.0) for side in (0, 1)]
    t = 0
    for out_ref in out_refs:
        for place in range(out_ref.shape[1] // LANES):
            total = low * tile_of(swap_ref, t) + sided(swap_pair, t, bit) * across(swap_ref, t, bit)
            total = total + sided(own_pair, t, bit) * across(own_ref, t, bit)
            out_ref[:, place * LANES : (place + 1) * LANES] = total
            t += 1


def later_ready_kernel(device_ref, bond_ref, swap_ref, *out_refs, middle, bond, scale):
    p, m, q = (bit_of(device_ref, middle + k) for k in (-1, 0, 1))
    low = jnp.where((p == m) & (q == m), strength_of(bond_ref, bond, scale), 0.0)
    first = 0
    for out_ref in out_refs:
        out_ref[...] = low * swap_ref[:, first : first + out_ref.shape[1]]
        first += out_ref.shape[1]


def later_sent_kernel(bond_ref, ready_ref, arrived_ref, out_ref, *, bond, scale):
    out_ref[...] = ready_ref[...] + strength_of(bond_ref, bond, scale) * arrived_ref[...]


def sent_kernel(device_ref, bond_ref, ready_ref, arrived_ref, out_ref, *, bond, scale):
    high = strength_of(bond_ref, bond + 2, scale)
    high = jnp.where(bit_of(device_ref, 0) != bit_of(device_ref, 1), high, 0.0)
    out_ref[...] = ready_ref[...] + high * arrived_ref[...]


def gather_kernel(device_ref, bond_ref, local_ref, first_ref, *refs, start, bit, local_bits, scale):
    out_ref = refs[-1]
    p, m, q = (bit_of(device_ref, k) for k in range(3))
    joint, low = (strength_of(bond_ref, local_bits - 1 + k, scale) for k in range(2))
    low = jnp.where((p != m) & (q == m), low, 0.0)
    halves = ((p == m) & (q == m)) | ((p != m) & (q != m))
    pair = [jnp.where(halves & (p != side), joint, 0.0) for side in (0, 1)]
    weights = []
    for k in range(len(refs) - 1):
        p, m, q = (bit_of(device_ref, 2 * k + j) for j in (2, 3, 4))
        weight = strength_of(bond_ref, local_bits + 2 * k + 2, scale)
        weights.append(jnp.where((p != m) & (q == m), weight, 0.0))
    for t in range(out_ref.shape[1] // LANES):
        total = tile_of(local_ref, start + t) + low * tile_of(first_ref, t)
        total = total + sided(pair, t, bit) * across(first_ref, t, bit)
        for weight, ref in zip(weights, refs):
            total = total + weight * tile_of(ref, t)
        out_ref[:, t * LANES : (t + 1) * LANES] = total


def packed(gram, vectors):
    fold = max(1, LANES // vectors)
    rows = vectors // fold
    return jnp.concatenate([gram[k * rows : (k + 1) * rows, :] for k in range(fold)], axis=1)


def unpacked(table, vectors):
    fold = max(1, LANES // vectors)
    return jnp.concatenate([table[:, k * vectors : (k + 1) * vectors] for k in range(fold)], axis=0)


def add_kernel(one_ref, two_ref, out_ref):
    out_ref[...] = one_ref[...] + two_ref[...]


def filter_kernel(before_ref, acc_ref, *refs, share, last):
    out_ref, gram_ref = refs[-2:]
    vectors, amp_count = acc_ref.shape
    table = before_ref[...]
    for first in range(0, amp_count, CHUNK):
        cols = slice(first, min(first + CHUNK, amp_count))
        total = acc_ref[:, cols]
        for ref in refs[:-2]:
            total = total + ref[:, cols]
        out_ref[:, cols] = total
        stacked = jnp.concatenate(pieces(total, 3), axis=0)
        table = table + lax.dot_general(
            stacked, stacked, (((1,), (1,)), ((), ())), preferred_element_type=jnp.float32
        )
    if not last:
        gram_ref[...] = table
        return

    def block(a, b):
        return table[a * vectors : (a + 1) * vectors, b * vectors : (b + 1) * vectors]

    gram = block(0, 0) + (block(0, 1) + block(1, 0)) + (block(1, 1) + (block(0, 2) + block(2, 0)))
    gram_ref[...] = packed(gram * share, vectors)


def reciprocal(values):
    guess = pl.reciprocal(values, approx=True)
    return guess * (2.0 - values * guess)


def factor(gram):
    vectors = gram.shape[0]
    lanes = max(LANES, 2 * vectors)
    rows = lax.broadcasted_iota(jnp.int32, (vectors, lanes), 0)
    cols = lax.broadcasted_iota(jnp.int32, (vectors, lanes), 1)
    rest = jnp.concatenate([gram, jnp.zeros((vectors, lanes - vectors), jnp.float32)], axis=1)
    rest = rest + (cols == rows + vectors).astype(jnp.float32)
    for panel in range(0, vectors, PANEL):
        columns = [jnp.broadcast_to(rest[:, k : k + 1], rest.shape) for k in range(panel, min(panel + PANEL, vectors))]
        for k in range(0, len(columns), 2):
            i, j = panel + k, panel + k + 1
            left, right = columns[k : k + 2]
            a, b, d = left[i:j, :], left[j : j + 1, :], right[j : j + 1, :]
            scale = reciprocal(a * d - b * b)
            left = jnp.where(rows > j, left, 0.0)
            right = jnp.where(rows > j, right, 0.0)

            def eliminate(values):
                one, two = values[i:j, :], values[j : j + 1, :]
                return values - (left * ((d * one - b * two) * scale) + right * ((a * two - b * one) * scale))

            columns[k + 2 :] = [eliminate(values) for values in columns[k + 2 :]]
            rest = eliminate(rest)
    diagonal = jnp.sum(jnp.where(cols == rows, rest, 0.0), axis=1, keepdims=True)
    odd = (rows & 1) == 1
    corner = jnp.sum(jnp.where((cols == rows - 1) & odd, rest, 0.0), axis=1, keepdims=True)
    before = pltpu.roll(rest, 1, 0)
    lead = pltpu.roll(jnp.broadcast_to(diagonal, rest.shape), 1, 0)
    ratio = jnp.where(odd, corner * reciprocal(lead), 0.0)
    rest = (rest - ratio * before) * lax.rsqrt(diagonal - corner * ratio)
    return jnp.where(cols >= rows, rest, 0.0)[:, :vectors], rest[:, vectors : 2 * vectors]


def finish_kernel(gram_ref, *refs):
    out_ref, upper_ref, held_ref, sems = refs[-4:]
    vectors = out_ref.shape[0]
    upper, inverse = factor(unpacked(gram_ref[...], vectors))
    upper_ref[...] = upper
    high, middle, low = pieces(inverse, 3)
    none = jnp.zeros_like(high)
    left = jnp.concatenate(
        [
            jnp.concatenate([high, high, high, low], axis=1),
            jnp.concatenate([middle, middle, none, none], axis=1),
        ],
        axis=0,
    )
    copies = []
    place = 0
    for ref in refs[:-4]:
        for first in range(0, ref.shape[1], OUT_CHUNK):
            count = min(OUT_CHUNK, ref.shape[1] - first)
            right = pieces(ref[:, first : first + count], 3)
            product = jnp.dot(left, jnp.concatenate(right + right[:1], axis=0), preferred_element_type=jnp.float32)
            held_ref[:, place : place + count] = product[:vectors] + product[vectors:]
            cols = pl.ds(place, count)
            copies.append(
                pltpu.make_async_copy(held_ref.at[:, cols], out_ref.at[:, cols], sems.at[len(copies)])
            )
            copies[-1].start()
            place += count
    for copy in copies:
        copy.wait()


def local(previous, current, field_levels, bond_levels, lo_bits):
    vectors, amp_count = current.shape
    site_count = field_levels.shape[0]
    devices = lax.axis_size("hi") * lax.axis_size("lo")
    local_bits = amp_count.bit_length() - 1
    global_bits = devices.bit_length() - 1
    rest_bits = local_bits - global_bits
    device = lax.axis_index("hi") * lax.axis_size("lo") + lax.axis_index("lo")
    place = device.astype(jnp.int32).reshape(1)
    scale = 4.0 / site_count
    whole = jax.ShapeDtypeStruct((vectors, amp_count), jnp.float32)
    size = vectors * amp_count
    vmem = pl.BlockSpec(memory_space=pltpu.VMEM)

    def permute(values, pairs):
        return lax.ppermute(values, AXES, pairs)

    def flips(mask, keep=lambda i: True):
        return [(i, i ^ mask) for i in range(devices) if keep(i)]

    def strength(bond):
        return (scale * 0.5 * COUPLING_STEP) * bond_levels[bond].astype(jnp.float32)

    middles = tuple(range(3, global_bits - 1, 2))
    width = amp_count // 32
    parts = [(0, 20), (20, 12)]
    swaps = [permute(current, flips(1 << m - 1)) for m in middles or (3,)]
    firsts, boths = [], []
    for start, count in parts:
        piece = cut(current, start * width, count * width)
        firsts.append(permute(piece, route(devices, 1, FIRST)))
        boths.append([permute(piece, route(devices, m, LATER_FIRST)) for m in middles])

    current, _ = lax.optimization_barrier((current, piece))

    here = pl.pallas_call(
        functools.partial(local_kernel, global_bits=global_bits, scale=scale),
        out_shape=whole,
        in_specs=[smem()] * 3 + [vmem] * 2,
        out_specs=vmem,
        compiler_params=params(),
        cost_estimate=cost(6 * size * GROUP, 12 * size),
        name="local_bonds",
    )(place, field_levels, bond_levels, current, previous)
    ready = pl.pallas_call(
        functools.partial(ready_kernel, bit=rest_bits - 1, bond=local_bits - 1, scale=scale),
        out_shape=tuple(jax.ShapeDtypeStruct((vectors, count * width), jnp.float32) for _, count in parts),
        in_specs=[smem()] * 2 + [vmem] * 2,
        out_specs=tuple(vmem for _ in parts),
        compiler_params=params(),
        cost_estimate=cost(6 * size, 12 * size),
        name="ready",
    )(place, bond_levels, current, swaps[0])
    later_ready = [
        pl.pallas_call(
            functools.partial(later_ready_kernel, middle=m, bond=local_bits + m - 1, scale=scale),
            out_shape=tuple(jax.ShapeDtypeStruct((vectors, count * width), jnp.float32) for _, count in parts),
            in_specs=[smem()] * 2 + [vmem],
            out_specs=tuple(vmem for _ in parts),
            compiler_params=params(),
            cost_estimate=cost(size, 8 * size),
            name=f"ready_{m}",
        )(place, bond_levels, swap)
        for m, swap in zip(middles, swaps)
    ]
    firsts[0], here, ready, later_ready = lax.optimization_barrier((firsts[0], here, ready, later_ready))
    if global_bits % 2 == 0:
        top = global_bits - 1
        moved = permute(current, flips(3 << top - 1, lambda i: (i >> top & 1) != (i >> top - 1 & 1)))
        here = here + strength(site_count - 2) * moved

    seconds, ons, accs, sents = [], [], [], []
    for number, ((start, count), first, both, base) in enumerate(zip(parts, firsts, boths, ready)):
        shape = jax.ShapeDtypeStruct((vectors, count * width), jnp.float32)
        part_size = vectors * count * width
        sent = pl.pallas_call(
            functools.partial(sent_kernel, bond=local_bits - 1, scale=scale),
            out_shape=shape,
            in_specs=[smem()] * 2 + [vmem] * 2,
            out_specs=vmem,
            compiler_params=params(),
            cost_estimate=cost(0, 0),
            name=f"sent_on_{start}",
        )(place, bond_levels, base, first)
        seconds.append(permute(sent, route(devices, 1, SECOND)))
        sents.append(sent)
        arrived = both
        if start == 0:
            arrived, sent = lax.optimization_barrier((both, sent))
        on = []
        for m, values, bases in zip(middles, arrived, later_ready):
            sent = pl.pallas_call(
                functools.partial(later_sent_kernel, bond=local_bits + m, scale=scale),
                out_shape=shape,
                in_specs=[smem()] + [vmem] * 2,
                out_specs=vmem,
                compiler_params=params(),
                cost_estimate=cost(0, 0),
                name=f"sent_{m}_{start}",
            )(bond_levels, bases[number], values)
            on.append(permute(sent, route(devices, m, LATER_SECOND)))
        ons.append(on)
    firsts, sents = lax.optimization_barrier((firsts, sents))
    for (start, count), first, both in zip(parts, firsts, boths):
        shape = jax.ShapeDtypeStruct((vectors, count * width), jnp.float32)
        part_size = vectors * count * width
        accs.append(
            pl.pallas_call(
                functools.partial(
                    gather_kernel, start=start * width // LANES, bit=rest_bits - 1, local_bits=local_bits, scale=scale
                ),
                out_shape=shape,
                in_specs=[smem()] * 2 + [vmem] * (2 + len(both)),
                out_specs=vmem,
                compiler_params=params(),
                cost_estimate=cost(0, 0),
                name=f"gather_first_{start}",
            )(place, bond_levels, here, first, *both)
        )

    fold = max(1, LANES // vectors)
    table = (vectors // fold, vectors * fold)
    square = (3 * vectors, 3 * vectors)
    filtered = []
    products = jnp.zeros(square, jnp.float32)
    for number, ((start, count), acc, second, on) in enumerate(zip(parts, accs, seconds, ons)):
        last = number == len(parts) - 1
        part_size = vectors * count * width
        second, products = lax.optimization_barrier((second, products))
        acc = pl.pallas_call(
            add_kernel,
            out_shape=jax.ShapeDtypeStruct((vectors, count * width), jnp.float32),
            in_specs=[vmem] * 2,
            out_specs=vmem,
            compiler_params=params(),
            cost_estimate=cost(0 if last else ADD_COST, 0),
            name=f"add_{start}",
        )(acc, second)
        done, products = pl.pallas_call(
            functools.partial(filter_kernel, share=1.0 / (amp_count * devices), last=last),
            out_shape=(
                jax.ShapeDtypeStruct((vectors, count * width), jnp.float32),
                jax.ShapeDtypeStruct(table if last else square, jnp.float32),
            ),
            in_specs=[vmem] * (2 + len(on)),
            out_specs=(vmem, vmem),
            compiler_params=params(),
            cost_estimate=cost(6 * part_size * vectors, 16 * part_size),
            name=f"filter_gram_{start}",
        )(products, acc, *on)
        filtered.append(done)
    gram = products

    hub = 1 << lo_bits
    upper = [1 << k for k in range(lo_bits + 1, global_bits)]
    steps = [[hub]]
    if len(upper) > 1:
        steps.append([upper[0] | hub, upper[1] | hub, upper[0] | upper[1] | hub])
        upper = upper[2:]
    steps += [[mask | hub] for mask in upper + [1 << k for k in range(lo_bits)]]
    for masks in steps:
        gram = gram + sum(permute(gram, flips(mask)) for mask in masks)

    chunks = sum(-(-values.shape[1] // OUT_CHUNK) for values in filtered)
    return pl.pallas_call(
        finish_kernel,
        out_shape=(whole, jax.ShapeDtypeStruct((vectors, vectors), jnp.float32)),
        in_specs=[vmem] * (1 + len(filtered)),
        out_specs=(pl.BlockSpec(memory_space=pltpu.HBM), vmem),
        scratch_shapes=[pltpu.VMEM((vectors, amp_count), jnp.float32), pltpu.SemaphoreType.DMA((chunks,))],
        compiler_params=params(),
        cost_estimate=cost(12 * size * vectors, 8 * size),
        name="factor_apply",
    )(gram, *filtered)


def solution(mesh):
    in_specs = (P(None, AXES), P(None, AXES), P(), P())
    out_specs = (P(None, AXES), P())
    lo_bits = mesh.shape["lo"].bit_length() - 1
    return jax.shard_map(
        functools.partial(local, lo_bits=lo_bits), mesh=mesh, in_specs=in_specs, out_specs=out_specs, check_vma=False
    )
```
